32 devices in a mesh: groups: 2 (over y), tiles: 4 (over z), band: 2 (over x), rep: 2 (over core).
Axes of the slice: x: 2, y: 2, z: 4, core: 2. Of those that a mesh axis runs over, the one named last changes fastest.
Arguments:
- features: bfloat16 [8, 16, 2, 16, 128], P(('groups', 'band'), 'tiles'), parts along dimension 0, may hold values from -6 to 6
- state: float32 [8, 16, 16, 16, 128], P(('groups', 'band'), 'tiles'), parts along dimension 0, may hold values from -3 to 3
- live: int32 [16], P('tiles'), may hold values from 0 to 1, as said below
- neighbours: int32 [16, 2], P('tiles'), may hold values from -1 to 15, as said below
- coarse_perm: int32 [4, 4], P('tiles'), may hold values from 0 to 3, as said below
- coarse_state: float32 [32, 16, 4, 32], P(('groups', 'tiles', 'band')), parts along dimension 0, may hold values from -3 to 3
- w_update: bfloat16 [9, 16, 18], replicated, may hold values from -0.5 to 0.5
- b_update: float32 [16], replicated, may hold values from -3 to 3
- w_reset: bfloat16 [9, 16, 18], replicated, may hold values from -0.5 to 0.5
- b_reset: float32 [16], replicated, may hold values from -3 to 3
- w_cand: bfloat16 [9, 16, 18], replicated, may hold values from -0.5 to 0.5
- b_cand: float32 [16], replicated, may hold values from -3 to 3
- u_pool: float32 [16, 16], replicated, may hold values from -1.5 to 1.5
- u_state: float32 [16, 16], replicated, may hold values from -1.5 to 1.5
- b_coarse: float32 [16], replicated, may hold values from -3 to 3
Outputs:
- new_state: float32 [8, 16, 16, 16, 128], P(('groups', 'band'), 'tiles', 'rep'), parts along dimension 0
- coarse_next: float32 [32, 16, 4, 32], P(('groups', 'tiles', 'band')), parts along dimension 0
The draws below stay inside these ranges and needn't reach their ends.
There are 2 independent parts, one for each index of `groups`. The reference program is written for one: setup_inputs(seed, part) draws one part's arguments, and reference() takes and returns one part's arrays. A program takes and returns all parts, laid end to end along the dimension named above; an argument that names none is the same for every part. Nothing has to cross between parts.
Inputs may be any that keep to these rules, and one draw needn't show every extreme that they name: Every device of tiles has between 1 and 4 live slots, at any positions; in every draw some device has all 4 live. `neighbours`: the live tiles form one vertical chain that passes the devices of tiles in index order, each device's live tiles forming one run of the chain in some order; entry 0 names the tile above, entry 1 the tile below, -1 at the chain's two ends and in both entries of an empty slot. `coarse_perm`: each row is a permutation of 0 to 3.
All inputs are finite; a program needn't handle non-finite values.
Results may differ from the reference program's by a relative error of at most 0.0013.
Values may be sent and summed in bfloat16 or wider, within the bound.
A program may use at most 64 MiB of HBM per device.

```python
import jax
import jax.numpy as jnp
from jax import lax

C = 16
XC = 2
TR = 16
W = 128
SLOTS = 4
BANDS = 4
SLOTS_ALL = 16
CR = 4
CW = 32
N_TILES = 4


def build_chain(key):
    k_count, k_busy, k_order = jax.random.split(jax.random.fold_in(key, 11), 3)
    counts = jax.random.randint(k_count, (N_TILES,), 1, SLOTS + 1).astype(jnp.int32)
    busiest = jax.random.randint(k_busy, (), 0, N_TILES).astype(jnp.int32)
    counts = jnp.where(jnp.arange(N_TILES, dtype=jnp.int32) == busiest, SLOTS, counts)
    orders = jax.vmap(lambda k: jax.random.permutation(k, SLOTS))(jax.random.split(k_order, N_TILES)).astype(jnp.int32)
    taken = jnp.arange(SLOTS, dtype=jnp.int32)[None, :] < counts[:, None]
    slot_of = (orders + jnp.arange(N_TILES, dtype=jnp.int32)[:, None] * SLOTS).reshape(-1).astype(jnp.int32)
    live_order = taken.reshape(-1)
    position = jnp.arange(SLOTS_ALL, dtype=jnp.int32)
    before = lax.cummax(jnp.where(live_order, position, -1), axis=0)
    prev = jnp.concatenate([jnp.array([-1], dtype=jnp.int32), before[:-1]])
    after = lax.cummin(jnp.where(live_order, position, SLOTS_ALL), axis=0, reverse=True)
    nxt = jnp.concatenate([after[1:], jnp.array([SLOTS_ALL], dtype=jnp.int32)])
    upper = jnp.where(live_order & (prev >= 0), slot_of[jnp.clip(prev, 0, SLOTS_ALL - 1)], -1)
    lower = jnp.where(live_order & (nxt < SLOTS_ALL), slot_of[jnp.clip(nxt, 0, SLOTS_ALL - 1)], -1)
    live = jnp.zeros((SLOTS_ALL,), jnp.int32).at[slot_of].set(live_order.astype(jnp.int32))
    pairs = jnp.stack([upper, lower], axis=1).astype(jnp.int32)
    neigh = jnp.full((SLOTS_ALL, 2), -1, jnp.int32).at[slot_of].set(pairs)
    return (live, neigh)


def draw_live(key, part):
    return build_chain(key)[0]


def draw_neighbours(key, part):
    return build_chain(key)[1]


def draw_coarse_perm(key, part):
    keys = jax.random.split(jax.random.fold_in(key, 23), N_TILES)
    return jax.vmap(lambda k: jax.random.permutation(k, SLOTS))(keys).astype(jnp.int32)


def block_levels(stream_key, shape, pieces, smallest, high):
    def one(axis_at, parts):
        heights = jax.random.uniform(jax.random.fold_in(jax.random.fold_in(stream_key, 6), axis_at), (parts,), jnp.float32, smallest / len(pieces), high / len(pieces))
        return jnp.repeat(jnp.exp(heights), shape[axis_at] // parts).reshape((-1,) + (1,) * (len(shape) - axis_at - 1))

    level = one(*pieces[0])
    for cut in pieces[1:]:
        level = level * one(*cut)
    return level


def normal_values(rng, shape, deviation, reach, cuts=(), kind=jnp.bfloat16):
    entries = deviation * jax.random.normal(rng, shape, jnp.float32)
    if cuts:
        entries = entries * block_levels(rng, shape, cuts, -0.22, 0.18)
    return jnp.clip(entries, -reach, reach).astype(kind)


def setup_inputs(seed: int = 0, part: int = 0) -> dict:
    arg_keys = jax.random.split(jax.random.key(seed), 16)
    part_keys = jax.random.split(jax.random.fold_in(arg_keys[15], part), 16)
    return {
        "features": normal_values(part_keys[0], (BANDS, SLOTS_ALL, XC, TR, W), 1.0, 6.0, ((0, 2), (1, 4))),
        "state": normal_values(part_keys[1], (BANDS, SLOTS_ALL, C, TR, W), 0.5, 3.0, ((0, 2), (1, 4)), jnp.float32),
        "live": draw_live(jax.random.fold_in(arg_keys[15], 71), part),
        "neighbours": draw_neighbours(jax.random.fold_in(arg_keys[15], 71), part),
        "coarse_perm": draw_coarse_perm(jax.random.fold_in(arg_keys[15], 71), part),
        "coarse_state": normal_values(part_keys[5], (SLOTS_ALL, C, CR, CW), 0.5, 3.0, ((0, 8),), jnp.float32),
        "w_update": normal_values(arg_keys[6], (9, C, C + XC), (9 * (C + XC)) ** -0.5, 0.5),
        "b_update": normal_values(arg_keys[7], (C,), 0.5, 3.0, (), jnp.float32),
        "w_reset": normal_values(arg_keys[8], (9, C, C + XC), (9 * (C + XC)) ** -0.5, 0.5),
        "b_reset": normal_values(arg_keys[9], (C,), 0.5, 3.0, (), jnp.float32),
        "w_cand": normal_values(arg_keys[10], (9, C, C + XC), (9 * (C + XC)) ** -0.5, 0.5),
        "b_cand": normal_values(arg_keys[11], (C,), 0.5, 3.0, (), jnp.float32),
        "u_pool": normal_values(arg_keys[12], (C, C), C ** -0.5, 1.5, (), jnp.float32),
        "u_state": normal_values(arg_keys[13], (C, C), C ** -0.5, 1.5, (), jnp.float32),
        "b_coarse": normal_values(arg_keys[14], (C,), 0.5, 3.0, (), jnp.float32),
    }


def pad_slots(arr, nbr, depth):
    row_count = arr.shape[2]
    ups = nbr[:, 0]
    downs = nbr[:, 1]
    top = jnp.take(arr[:, :, row_count - depth:, :], jnp.clip(ups, 0, arr.shape[0] - 1), axis=0)
    top = jnp.where((ups >= 0)[:, None, None, None], top, jnp.zeros_like(top))
    bottom = jnp.take(arr[:, :, :depth, :], jnp.clip(downs, 0, arr.shape[0] - 1), axis=0)
    bottom = jnp.where((downs >= 0)[:, None, None, None], bottom, jnp.zeros_like(bottom))
    full = jnp.concatenate([top, arr, bottom], axis=2)
    return jnp.pad(full, ((0, 0), (0, 0), (0, 0), (2, 2)))


def apply_filter(padded_input, filter_weight, dilation_rate, row_count, column_count):
    total = jnp.zeros((padded_input.shape[0], filter_weight.shape[1], row_count, column_count), jnp.float32)
    for left_operand in (-1, 0, 1):
        for right_operand in (-1, 0, 1):
            window_slice = padded_input[:, :, 2 + left_operand * dilation_rate:2 + left_operand * dilation_rate + row_count, 2 + right_operand * dilation_rate:2 + right_operand * dilation_rate + column_count]
            weight = filter_weight[(left_operand + 1) * 3 + (right_operand + 1)].astype(jnp.float32)
            total = total + jnp.einsum('oi,sirw->sorw', weight, window_slice.astype(jnp.float32))
    return total


def reference(features, state, live, neighbours, coarse_perm, coarse_state, w_update, b_update, w_reset, b_reset, w_cand, b_cand, u_pool, u_state, b_coarse):
    row_count = state.shape[3]
    column_count = state.shape[4]
    alive = live.astype(jnp.float32)[:, None, None, None]

    def one_band(pair):
        feats, hidden = pair
        hb = hidden.astype(jnp.bfloat16)
        joined = jnp.concatenate([feats, hb], axis=1)
        first = pad_slots(joined, neighbours, 2)
        update = jax.nn.sigmoid(apply_filter(first, w_update, 1, row_count, column_count) + b_update[:, None, None])
        reset = jax.nn.sigmoid(apply_filter(first, w_reset, 1, row_count, column_count) + b_reset[:, None, None])
        gated = (reset * hb.astype(jnp.float32)).astype(jnp.bfloat16)
        second = pad_slots(jnp.concatenate([feats, gated], axis=1), neighbours, 2)
        candidate = jnp.tanh(apply_filter(second, w_cand, 2, row_count, column_count) + b_cand[:, None, None])
        return ((1.0 - update) * hidden + update * candidate) * alive

    new_state = lax.map(one_band, (features, state))
    slots = state.shape[1]
    chans = state.shape[2]
    summed = jnp.sum(new_state, axis=0)
    pooled = summed.reshape(slots, chans, row_count // 4, 4, column_count // 4, 4).sum(axis=(3, 5)) / 16.0
    tiles_count = coarse_perm.shape[0]
    per = coarse_perm.shape[1]
    source = (jnp.arange(tiles_count, dtype=jnp.int32)[:, None] * per + coarse_perm).reshape(-1).astype(jnp.int32)
    picked = jnp.take(pooled, source, axis=0)
    pre = jnp.einsum('oc,kcij->koij', u_pool, picked, precision=lax.Precision.HIGHEST)
    pre = pre + jnp.einsum('oc,kcij->koij', u_state, coarse_state, precision=lax.Precision.HIGHEST)
    pre = pre + b_coarse[None, :, None, None]
    coarse_next = coarse_state + jnp.tanh(pre)
    return new_state, coarse_next
```

```python
import functools

import jax
import jax.numpy as jnp
from jax import lax
from jax.experimental import pallas as pl
from jax.experimental.pallas import tpu as pltpu
from jax.sharding import PartitionSpec as P

MESH = pl.DeviceIdType.MESH
HIGHEST = lax.Precision.HIGHEST
F32 = jnp.float32
BF16 = jnp.bfloat16


def iota(shape, dim):
    return lax.broadcasted_iota(jnp.int32, shape, dim)


def sigmoid(x):
    return 0.5 * jnp.tanh(0.5 * x) + 0.5


def shifted(x, step):
    width = x.shape[1]
    wide = pltpu.roll(x.astype(F32), (-step) % width, 1)
    column = iota(x.shape, 1) + step
    return jnp.where((column >= 0) & (column < width), wide, 0.0).astype(BF16)


def kernel(
    nt, nb, nr,
    features, state, live, nbrs, perm, cs, wu, bu, wr, br, wc, bc, u_pool, u_state, b_coarse,
    out, cout,
    mains, tops, bots, send_up, send_dn, wexp, t1, t2, x1, x2, parts, csl,
    up_sems, dn_sems, pool_send, pool_recv,
):
    bands, slots, chans, rows, cols = state.shape
    ins = features.shape[2]
    half = chans // nr
    width = ins + chans
    own, cw = cs.shape[0], cs.shape[3]
    km, kh = width * rows, width * 8
    ks = km + 2 * kh
    kt = 3 * ks
    tile = lax.axis_index("tiles")
    band = lax.axis_index("band")
    rep = lax.axis_index("rep")
    base = tile * slots
    npeer = nb * nr
    me = band * nr + rep
    start = rep * half

    barrier = pltpu.get_barrier_semaphore()

    @pl.when(tile > 0)
    def _():
        pl.semaphore_signal(barrier, inc=1, device_id={"tiles": tile - 1}, device_id_type=MESH)

    @pl.when(tile < nt - 1)
    def _():
        pl.semaphore_signal(barrier, inc=1, device_id={"tiles": tile + 1}, device_id_type=MESH)

    for d in range(1, npeer):
        peer = lax.rem(me + d, npeer)
        pl.semaphore_signal(
            barrier, inc=1, device_id={"band": peer // nr, "rep": lax.rem(peer, nr)}, device_id_type=MESH
        )

    first = jnp.int32(0)
    last = jnp.int32(0)
    for s in range(slots):
        u, d = nbrs[s, 0], nbrs[s, 1]
        alive = live[s] > 0
        first = jnp.where(alive & ((u < base) | (u >= base + slots)), s, first)
        last = jnp.where(alive & ((d < base) | (d >= base + slots)), s, last)
    for b in range(bands):
        f, h = features[b, first].astype(F32)[:, :8], state[b, first, :, :8]
        send_up[b] = jnp.concatenate([f, h], axis=0).reshape(kh, cols).astype(BF16)
        f, h = features[b, last].astype(F32)[:, rows - 8 :], state[b, last, :, rows - 8 :]
        send_dn[b] = jnp.concatenate([f, h], axis=0).reshape(kh, cols).astype(BF16)

    has_up, has_dn = tile > 0, tile < nt - 1
    pl.semaphore_wait(barrier, npeer - 1 + jnp.where(has_up, 1, 0) + jnp.where(has_dn, 1, 0))

    def copy_up():
        return pltpu.make_async_remote_copy(
            send_up, tops.at[slots], up_sems.at[0], up_sems.at[1],
            device_id={"tiles": tile - 1}, device_id_type=MESH,
        )

    def copy_dn():
        return pltpu.make_async_remote_copy(
            send_dn, bots.at[slots], dn_sems.at[0], dn_sems.at[1],
            device_id={"tiles": tile + 1}, device_id_type=MESH,
        )

    @pl.when(has_up)
    def _():
        copy_up().start()

    @pl.when(has_dn)
    def _():
        copy_dn().start()

    @pl.when(jnp.logical_not(has_up))
    def _():
        bots[slots] = jnp.zeros((bands, kh, cols), BF16)

    @pl.when(jnp.logical_not(has_dn))
    def _():
        tops[slots] = jnp.zeros((bands, kh, cols), BF16)

    for s in range(slots):
        for b in range(bands):
            f = features[b, s].astype(F32)
            h = state[b, s]
            j = jnp.concatenate([f, h], axis=0)
            mains[s, b] = j.reshape(km, cols).astype(BF16)
            tops[s, b] = j[:, :8].reshape(kh, cols).astype(BF16)
            bots[s, b] = j[:, rows - 8 :].reshape(kh, cols).astype(BF16)
    tops[slots + 1] = jnp.zeros((bands, kh, cols), BF16)
    bots[slots + 1] = jnp.zeros((bands, kh, cols), BF16)

    def lanes(shape):
        k = iota(shape, len(shape) - 1)
        side = (k >= ks).astype(jnp.int32) + (k >= 2 * ks).astype(jnp.int32)
        q = k - ks * side
        up, dn = q >= km, q >= km + kh
        hq = jnp.where(dn, q - (km + kh), q - km)
        chan = jnp.where(up, hq >> 3, q >> 4)
        row = jnp.where(up, (hq & 7) + jnp.where(dn, rows, -8), q & (rows - 1))
        return side, chan, row

    side, chan, _ = lanes((width, kt))
    spread = jnp.zeros((9 * chans, kt), F32)
    for b in range(3):
        stack = jnp.concatenate([w[3 * a + b] for w in (wu, wr, wc) for a in range(3)], axis=0)
        pick = ((side == b) & (chan == iota((width, kt), 0))).astype(F32).astype(BF16)
        spread = spread + jnp.dot(stack, pick, preferred_element_type=F32)
    wexp[...] = spread.reshape(9, chans, kt)

    def fill(target, at, gate, outs, count, first_row, dilation):
        _, _, row = lanes((count, kt))
        delta = row - (iota((count, kt), 0) + first_row)
        hits = [delta == a * dilation for a in (-1, 0, 1)]

        def step(o, carry):
            total = jnp.zeros((count, kt), F32)
            for a in range(3):
                total = jnp.where(hits[a], wexp[3 * gate + a, pl.ds(outs + o, 1), :], total)
            target[pl.ds(pl.multiple_of(at + o * count, count), count), :] = total.astype(BF16)
            return carry

        return step

    def fill_halo(at, first_row):
        _, _, row = lanes((16, kt))
        which = iota((16, kt), 0)
        delta = row - ((which & 7) + first_row)
        hits = [delta == a for a in (-1, 0, 1)]

        def step(o, carry):
            total = jnp.zeros((16, kt), F32)
            for a in range(3):
                lo = wexp[3 + a, pl.ds(2 * o, 1), :]
                hi = wexp[3 + a, pl.ds(2 * o + 1, 1), :]
                total = jnp.where(hits[a], jnp.where(which < 8, lo, hi), total)
            t1[pl.ds(pl.multiple_of(at + o * 16, 16), 16), :] = total.astype(BF16)
            return carry

        return step

    mu = half * rows
    lax.fori_loop(0, half, fill(t1, 0, 0, start, rows, 0, 1), 0)
    lax.fori_loop(0, chans, fill(t1, mu, 1, 0, rows, 0, 1), 0)
    lax.fori_loop(0, chans // 2, fill_halo(mu + chans * rows, -8), 0)
    lax.fori_loop(0, chans // 2, fill_halo(mu + chans * rows + chans * 8, rows), 0)
    lax.fori_loop(0, half, fill(t2, 0, 2, start, rows, 0, 2), 0)

    csl[...] = jnp.zeros_like(csl)
    for k in range(own):
        for i in range(cs.shape[2]):
            csl[:, i * cols + k * cw : i * cols + (k + 1) * cw] = cs[k, :, i, :]
    coarse_bias = jnp.zeros((chans, 1), F32)
    for o in range(chans):
        coarse_bias = jnp.where(iota((chans, 1), 0) == o, b_coarse[o], coarse_bias)

    @pl.when(has_up)
    def _():
        copy_up().wait_send()

    @pl.when(has_dn)
    def _():
        copy_up().wait_recv()

    @pl.when(has_dn)
    def _():
        copy_dn().wait_send()

    @pl.when(has_up)
    def _():
        copy_dn().wait_recv()

    def place(s, side):
        n = nbrs[s, side]
        here = (n >= base) & (n < base + slots)
        return jnp.where(here, n - base, jnp.where(n >= 0, slots, slots + 1))

    def one_slot(s, pooled):
        above, below = place(s, 0), place(s, 1)
        pieces = []
        for b in range(bands):
            main, up, dn = mains[s, b], bots[above, b], tops[below, b]
            pieces.append((main, up, dn))
            x = jnp.concatenate([main, up, dn], axis=0)
            at = slice(b * cols, (b + 1) * cols)
            x1[0:ks, at] = shifted(x, -1)
            x1[ks : 2 * ks, at] = x
            x1[2 * ks :, at] = shifted(x, 1)
        acc = jnp.dot(t1[...], x1[...], preferred_element_type=F32)
        fm, fh = ins * rows, ins * 8
        for b in range(bands):
            at = slice(b * cols, (b + 1) * cols)
            main, up, dn = pieces[b]
            parts2 = []
            row = mu
            for piece, skip, count in ((main, fm, rows), (up, fh, 8), (dn, fh, 8)):
                held = piece.astype(F32)
                parts2.append(held[:skip])
                for o in range(chans):
                    reset = sigmoid(acc[row : row + count, at] + br[o])
                    parts2.append(reset * held[skip + o * count : skip + (o + 1) * count])
                    row += count
            x = jnp.concatenate(parts2, axis=0).astype(BF16)
            x2[0:ks, at] = shifted(x, -2)
            x2[ks : 2 * ks, at] = x
            x2[2 * ks :, at] = shifted(x, 2)
        acc2 = jnp.dot(t2[...], x2[...], preferred_element_type=F32)
        scale = live[s].astype(F32)
        summed = []
        for o in range(half):
            both = None
            for b in range(bands):
                at = slice(b * cols, (b + 1) * cols)
                update = sigmoid(acc[o * rows : (o + 1) * rows, at] + bu[start + o])
                cand = jnp.tanh(acc2[o * rows : (o + 1) * rows, at] + bc[start + o])
                new = ((1.0 - update) * state[b, s, start + o] + update * cand) * scale
                out[b, s, o] = new
                both = new if both is None else both + new
            summed.append(both)
        summed = jnp.concatenate(summed, axis=0)
        spot = jnp.int32(0)
        for k in range(slots):
            spot = jnp.where(perm[0, k] == s, k, spot)
        gather = jnp.where(
            iota((cols, slots * cw), 1) == spot * cw + (iota((cols, slots * cw), 0) >> 2), 1.0 / 16.0, 0.0
        )
        return pooled + jnp.dot(summed, gather, precision=HIGHEST, preferred_element_type=F32)

    pooled = lax.fori_loop(0, slots, one_slot, jnp.zeros((mu, slots * cw), F32))
    cr = rows // 4
    m, q = iota((cr * half, mu), 0), iota((cr * half, mu), 1)
    rowsum = jnp.where(((m % half) == (q >> 4)) & ((m // half) == ((q & (rows - 1)) >> 2)), 1.0, 0.0)
    parts[me] = jnp.dot(rowsum, pooled, precision=HIGHEST, preferred_element_type=F32)

    copies = []
    for d in range(1, npeer):
        peer = lax.rem(me + d, npeer)
        copy = pltpu.make_async_remote_copy(
            parts.at[me], parts.at[me], pool_send.at[d - 1], pool_recv.at[d - 1],
            device_id={"band": peer // nr, "rep": lax.rem(peer, nr)}, device_id_type=MESH,
        )
        copy.start()
        copies.append(copy)
    held = csl[...]
    pre = jnp.dot(u_state[...], held, precision=HIGHEST, preferred_element_type=F32) + coarse_bias
    for copy in copies:
        copy.wait()
    halves = []
    for r in range(nr):
        total = parts[r]
        for b in range(1, nb):
            total = total + parts[b * nr + r]
        halves.append(pltpu.roll(total, lax.rem(slots * cw - band * (own * cw), slots * cw), 1))
    wide = jnp.concatenate(
        [jnp.concatenate([x[i * half : (i + 1) * half] for x in halves], axis=0) for i in range(cr)], axis=1
    )
    pre = pre + jnp.dot(u_pool[...], wide, precision=HIGHEST, preferred_element_type=F32)
    new = held + jnp.tanh(pre)
    for k in range(own):
        for i in range(cr):
            cout[k, :, i, :] = new[:, i * cols + k * cw : i * cols + (k + 1) * cw]


def shards(nt, nb, nr, features, state, live, nbrs, perm, cs, wu, bu, wr, br, wc, bc, u_pool, u_state, b_coarse):
    bands, slots, chans, rows, cols = state.shape
    width = features.shape[2] + chans
    half = chans // nr
    km, kh = width * rows, width * 8
    kt = 3 * (km + 2 * kh)
    cr = rows // 4
    vm = pl.BlockSpec(memory_space=pltpu.VMEM)
    sm = pl.BlockSpec(memory_space=pltpu.SMEM)
    return pl.pallas_call(
        functools.partial(kernel, nt, nb, nr),
        out_shape=(
            jax.ShapeDtypeStruct((bands, slots, half, rows, cols), F32),
            jax.ShapeDtypeStruct(cs.shape, F32),
        ),
        in_specs=[vm, vm, sm, sm, sm, vm, vm, sm, vm, sm, vm, sm, vm, vm, sm],
        out_specs=(vm, vm),
        scratch_shapes=[
            pltpu.VMEM((slots, bands, km, cols), BF16),
            pltpu.VMEM((slots + 2, bands, kh, cols), BF16),
            pltpu.VMEM((slots + 2, bands, kh, cols), BF16),
            pltpu.VMEM((bands, kh, cols), BF16),
            pltpu.VMEM((bands, kh, cols), BF16),
            pltpu.VMEM((9, chans, kt), F32),
            pltpu.VMEM((half * rows + chans * (rows + 16), kt), BF16),
            pltpu.VMEM((half * rows, kt), BF16),
            pltpu.VMEM((kt, bands * cols), BF16),
            pltpu.VMEM((kt, bands * cols), BF16),
            pltpu.VMEM((nb * nr, cr * half, cols), F32),
            pltpu.VMEM((chans, cr * cols), F32),
            pltpu.SemaphoreType.DMA((2,)),
            pltpu.SemaphoreType.DMA((2,)),
            pltpu.SemaphoreType.DMA((nb * nr - 1,)),
            pltpu.SemaphoreType.DMA((nb * nr - 1,)),
        ],
        compiler_params=pltpu.CompilerParams(
            collective_id=0, has_side_effects=True, vmem_limit_bytes=40 * 1024 * 1024
        ),
    )(features, state, live, nbrs, perm, cs, wu, bu, wr, br, wc, bc, u_pool, u_state, b_coarse)


def solution(mesh):
    nt, nb, nr = mesh.shape["tiles"], mesh.shape["band"], mesh.shape["rep"]
    return jax.shard_map(
        functools.partial(shards, nt, nb, nr),
        mesh=mesh,
        in_specs=(
            P(("groups", "band"), "tiles", None, None, None),
            P(("groups", "band"), "tiles", None, None, None),
            P("tiles"),
            P("tiles", None),
            P("tiles", None),
            P(("groups", "tiles", "band"), None, None, None),
            P(),
            P(),
            P(),
            P(),
            P(),
            P(),
            P(),
            P(),
            P(),
        ),
        out_specs=(
            P(("groups", "band"), "tiles", "rep", None, None),
            P(("groups", "tiles", "band"), None, None, None),
        ),
        check_vma=False,
    )
```

```python
import functools

import jax
import jax.numpy as jnp
from jax import lax
from jax.experimental import pallas as pl
from jax.experimental.pallas import tpu as pltpu
from jax.sharding import PartitionSpec as P

MESH = pl.DeviceIdType.MESH
HIGHEST = lax.Precision.HIGHEST
F32 = jnp.float32
BF16 = jnp.bfloat16


def iota(shape, dim):
    return lax.broadcasted_iota(jnp.int32, shape, dim)


def sigmoid(x):
    return 0.5 * jnp.tanh(0.5 * x) + 0.5


def shifted(x, step):
    width = x.shape[1]
    wide = pltpu.roll(x, (-step) % width, 1)
    column = iota(x.shape, 1) + step
    return jnp.where((column >= 0) & (column < width), wide, jnp.zeros_like(wide))


def kernel(
    nt, nb, nr, ins, rows,
    live, nbrs, perm, bu, br, bc, b_coarse, features_in, state_in, cs_in, wu_in, wr_in, wc_in, u_pool_in, u_state_in,
    out, cout,
    features, state, cs, wu, wr, wc, u_pool, u_state,
    feats, send_up, send_dn, got_up, got_dn, tops, bots, gtops, gbots, strip, gates,
    w1, w2, w3, t1, t2, t3, x1, x2, parts, csl,
    load_sems, up_sems, dn_sems, pool_send, pool_recv,
):
    bands, slots, flat, cols = state.shape
    chans = flat // rows
    half = chans // nr
    width = ins + chans
    own, cr, cw = cs.shape[0], cs.shape[2], cs.shape[3]
    km = width * rows
    slab = strip.shape[0] // 12
    tile = lax.axis_index("tiles")
    band = lax.axis_index("band")
    rep = lax.axis_index("rep")
    base = tile * slots
    npeer = nb * nr
    me = band * nr + rep
    start = rep * half

    loads = [
        pltpu.make_async_copy(src, dst, load_sems.at[i])
        for i, (src, dst) in enumerate(
            (
                (state_in, state), (features_in, features), (wu_in, wu), (wr_in, wr), (wc_in, wc),
                (cs_in, cs), (u_pool_in, u_pool), (u_state_in, u_state),
            )
        )
    ]
    for load in loads:
        load.start()

    barrier = pltpu.get_barrier_semaphore()
    has_up, has_dn = tile > 0, tile < nt - 1

    @pl.when(has_up)
    def _():
        pl.semaphore_signal(barrier, inc=1, device_id={"tiles": tile - 1}, device_id_type=MESH)

    @pl.when(has_dn)
    def _():
        pl.semaphore_signal(barrier, inc=1, device_id={"tiles": tile + 1}, device_id_type=MESH)

    for d in range(1, npeer):
        peer = lax.rem(me + d, npeer)
        pl.semaphore_signal(
            barrier, inc=1, device_id={"band": peer // nr, "rep": lax.rem(peer, nr)}, device_id_type=MESH
        )

    first = jnp.int32(0)
    last = jnp.int32(0)
    for s in range(slots):
        u, d = nbrs[0, s], nbrs[1, s]
        alive = live[s] > 0
        first = jnp.where(alive & ((u < base) | (u >= base + slots)), s, first)
        last = jnp.where(alive & ((d < base) | (d >= base + slots)), s, last)

    loads[0].wait()
    loads[1].wait()
    for s in range(slots):
        for b in range(bands):
            feats[b, s] = features[b, s].astype(F32)

    blank = jnp.zeros((slab - width, cols), F32)

    def feat_rows(b, s, row):
        return jnp.concatenate([feats[b, s, ch * rows + row : ch * rows + row + 1] for ch in range(ins)] + [blank], axis=0)

    def row_slab(b, s, row):
        return jnp.concatenate([state[b, s, pl.ds(row, chans, stride=rows), :], feat_rows(b, s, row)], axis=0).astype(BF16)

    for b in range(bands):
        for i in range(3):
            send_up[b, i] = row_slab(b, first, i)
            send_dn[b, i] = row_slab(b, last, rows - 3 + i)

    pl.semaphore_wait(barrier, npeer - 1 + jnp.where(has_up, 1, 0) + jnp.where(has_dn, 1, 0))

    def copy_up():
        return pltpu.make_async_remote_copy(
            send_up, got_dn, up_sems.at[0], up_sems.at[1], device_id={"tiles": tile - 1}, device_id_type=MESH
        )

    def copy_dn():
        return pltpu.make_async_remote_copy(
            send_dn, got_up, dn_sems.at[0], dn_sems.at[1], device_id={"tiles": tile + 1}, device_id_type=MESH
        )

    @pl.when(has_up)
    def _():
        copy_up().start()

    @pl.when(has_dn)
    def _():
        copy_dn().start()

    @pl.when(jnp.logical_not(has_up))
    def _():
        got_up[...] = jnp.zeros_like(got_up)

    @pl.when(jnp.logical_not(has_dn))
    def _():
        got_dn[...] = jnp.zeros_like(got_dn)

    def lanes(shape, main, halo):
        size = main + slab * len(halo)
        k = iota(shape, 1)
        side = (k >= size).astype(jnp.int32) + (k >= 2 * size).astype(jnp.int32)
        q = k - size * side
        h = q - main
        chan = jnp.where(h >= 0, h & (slab - 1), q >> 4)
        row = q & (rows - 1)
        for j, at in enumerate(halo):
            row = jnp.where(h >= j * slab, at, row)
        entry = jnp.where(chan < chans, chan + ins, chan - chans)
        return side, jnp.where(chan < width, entry, -1), row

    def spread(target, weights, main, halo):
        shape = (width, target.shape[2])
        side, entry, _ = lanes(shape, main, halo)
        total = jnp.zeros((3 * chans * len(weights), shape[1]), F32)
        for b in range(3):
            stack = jnp.concatenate([w[3 * a + b] for w in weights for a in range(3)], axis=0)
            pick = ((side == b) & (entry == iota(shape, 0))).astype(F32).astype(BF16)
            total = total + jnp.dot(stack, pick, preferred_element_type=F32)
        target[...] = total.reshape(target.shape)

    def fill(target, at, source, gate, outs, count, main, halo, dilation):
        shape = (rows, target.shape[1])
        _, _, row = lanes(shape, main, halo)
        delta = row - iota(shape, 0)
        hits = [(delta == a * dilation).astype(F32).astype(BF16) for a in (-1, 0, 1)]

        def step(o, carry):
            total = None
            for a in range(3):
                line = jnp.broadcast_to(source[3 * gate + a, pl.ds(outs + o, 1), :], shape).astype(BF16)
                total = line * hits[a] if total is None else total + line * hits[a]
            target[pl.ds(pl.multiple_of(at + o * rows, rows), rows), :] = total
            return carry

        lax.fori_loop(0, count, step, 0)

    mu = half * rows
    halo1, halo2, halo3 = (-1, rows), (-2, -1, rows, rows + 1), (-3, -2, -1, 0)
    for load in loads[2:5]:
        load.wait()
    spread(w1, (wu, wr), km, halo1)
    spread(w2, (wc,), km, halo2)
    spread(w3, (wr,), 0, halo3)
    fill(t1, 0, w1, 0, start, half, km, halo1, 1)
    fill(t1, mu, w1, 1, 0, chans, km, halo1, 1)
    fill(t2, 0, w2, 0, start, half, km, halo2, 2)
    _, _, row3 = lanes((chans, t3.shape[1]), 0, halo3)
    for i in range(2):
        total = jnp.zeros((chans, t3.shape[1]), F32)
        for a in range(3):
            total = jnp.where(row3 == i - 2 + a - 1, w3[a], total)
        t3[i * chans : (i + 1) * chans] = total.astype(BF16)

    for load in loads[5:]:
        load.wait()
    csl[...] = jnp.zeros_like(csl)
    for k in range(own):
        for i in range(cr):
            csl[:, i * cols + k * cw : i * cols + (k + 1) * cw] = cs[k, :, i, :]
    coarse_bias = jnp.zeros((chans, 1), F32)
    for o in range(chans):
        coarse_bias = jnp.where(iota((chans, 1), 0) == o, b_coarse[o], coarse_bias)

    k1, k2 = km + 2 * slab, km + 4 * slab
    for s in range(slots):
        for b in range(bands):
            at = slice(b * cols, (b + 1) * cols)
            tops[s, b] = row_slab(b, s, 0)
            bots[s, b] = row_slab(b, s, rows - 1)
            x = state[b, s].astype(BF16)
            f = features[b, s]
            for j, step in enumerate((-1, 0, 1)):
                x1[s, j * k1 : j * k1 + flat, at] = shifted(x, step) if step else x
                x1[s, j * k1 + flat : j * k1 + km, at] = shifted(f, step) if step else f
                x2[s, j * k2 + flat : j * k2 + km, at] = shifted(f, 2 * step) if step else f
    tops[slots + 1] = jnp.zeros((bands, slab, cols), BF16)
    bots[slots + 1] = jnp.zeros((bands, slab, cols), BF16)
    gtops[slots + 1] = jnp.zeros((bands, 2, slab, cols), BF16)
    gbots[slots + 1] = jnp.zeros((bands, 2, slab, cols), BF16)
    edge_up = [row_slab(b, first, 0) for b in range(bands)]
    edge_dn = [row_slab(b, last, rows - 1) for b in range(bands)]

    @pl.when(has_up)
    def _():
        copy_up().wait_send()

    @pl.when(has_dn)
    def _():
        copy_up().wait_recv()

    @pl.when(has_dn)
    def _():
        copy_dn().wait_send()

    @pl.when(has_up)
    def _():
        copy_dn().wait_recv()

    for b in range(bands):
        bots[slots, b] = got_up[b, 2]
        tops[slots, b] = got_dn[b, 0]
        for side in range(2):
            four = [got_up[b, i] for i in range(3)] + [edge_up[b]] if side == 0 else [edge_dn[b]] + [got_dn[b, i] for i in range(3)]
            at = slice((2 * side + b) * cols, (2 * side + b + 1) * cols)
            x = jnp.concatenate(four, axis=0)
            strip[0 : 4 * slab, at] = shifted(x, -1)
            strip[4 * slab : 8 * slab, at] = x
            strip[8 * slab :, at] = shifted(x, 1)
    acc = jnp.dot(t3[...], strip[...], preferred_element_type=F32)
    reset_bias = jnp.zeros((chans, 1), F32)
    for o in range(chans):
        reset_bias = jnp.where(iota((chans, 1), 0) == o, br[o], reset_bias)
    for b in range(bands):
        for side in range(2):
            at = slice((2 * side + b) * cols, (2 * side + b + 1) * cols)
            for i in range(2):
                held = (got_up[b, 1 + i] if side == 0 else got_dn[b, i]).astype(F32)
                reset = sigmoid(acc[i * chans : (i + 1) * chans, at] + reset_bias)
                joined = jnp.concatenate([reset * held[:chans], held[chans:]], axis=0).astype(BF16)
                if side == 0:
                    gbots[slots, b, i] = joined
                else:
                    gtops[slots, b, i] = joined

    def place(s, side):
        n = nbrs[side, s]
        here = (n >= base) & (n < base + slots)
        return jnp.where(here, n - base, jnp.where(n >= 0, slots, slots + 1))

    updates = []
    for s in range(slots):
        above, below = place(s, 0), place(s, 1)
        for b in range(bands):
            at = slice(b * cols, (b + 1) * cols)
            x = jnp.concatenate([bots[above, b], tops[below, b]], axis=0)
            for j, step in enumerate((-1, 0, 1)):
                x1[s, j * k1 + km : (j + 1) * k1, at] = shifted(x, step) if step else x
        acc = jnp.dot(t1[...], x1[s], preferred_element_type=F32)
        for b in range(bands):
            at = slice(b * cols, (b + 1) * cols)
            for o in range(half):
                gates[s, b, o * rows : (o + 1) * rows] = sigmoid(acc[o * rows : (o + 1) * rows, at] + bu[start + o])
            for o in range(chans):
                reset = sigmoid(acc[mu + o * rows : mu + (o + 1) * rows, at] + br[o])
                held = state[b, s, o * rows : (o + 1) * rows].astype(BF16).astype(F32)
                gates[s, b, mu + o * rows : mu + (o + 1) * rows] = reset * held
            x = gates[s, b, mu:].astype(BF16)
            for j, step in enumerate((-1, 0, 1)):
                x2[s, j * k2 : j * k2 + flat, at] = shifted(x, 2 * step) if step else x
            for i in range(2):
                for target, row in ((gtops, i), (gbots, rows - 2 + i)):
                    g = gates[s, b, pl.ds(mu + row, chans, stride=rows), :]
                    target[s, b, i] = jnp.concatenate([g, feat_rows(b, s, row)], axis=0).astype(BF16)

    pooled = jnp.zeros((mu, slots * cw), F32)
    for s in range(slots):
        above, below = place(s, 0), place(s, 1)
        for b in range(bands):
            at = slice(b * cols, (b + 1) * cols)
            x = jnp.concatenate([gbots[above, b, 0], gbots[above, b, 1], gtops[below, b, 0], gtops[below, b, 1]], axis=0)
            for j, step in enumerate((-1, 0, 1)):
                x2[s, j * k2 + km : (j + 1) * k2, at] = shifted(x, 2 * step) if step else x
        acc = jnp.dot(t2[...], x2[s], preferred_element_type=F32)
        scale = live[s].astype(F32)
        summed = []
        for o in range(half):
            both = None
            for b in range(bands):
                at = slice(b * cols, (b + 1) * cols)
                update = gates[s, b, o * rows : (o + 1) * rows]
                cand = jnp.tanh(acc[o * rows : (o + 1) * rows, at] + bc[start + o])
                held = state[b, s, pl.ds(pl.multiple_of((start + o) * rows, rows), rows), :]
                new = ((1.0 - update) * held + update * cand) * scale
                out[b, s, o] = new
                both = new if both is None else both + new
            summed.append(both)
        summed = jnp.concatenate(summed, axis=0)
        spot = jnp.int32(0)
        for k in range(slots):
            spot = jnp.where(perm[0, k] == s, k, spot)
        gather = jnp.where(
            iota((cols, slots * cw), 1) == spot * cw + (iota((cols, slots * cw), 0) >> 2), 1.0 / 16.0, 0.0
        )
        pooled = pooled + jnp.dot(summed, gather, precision=HIGHEST, preferred_element_type=F32)

    m, q = iota((cr * half, mu), 0), iota((cr * half, mu), 1)
    rowsum = jnp.where(((m % half) == (q >> 4)) & ((m // half) == ((q & (rows - 1)) >> 2)), 1.0, 0.0)
    parts[me] = jnp.dot(rowsum, pooled, precision=HIGHEST, preferred_element_type=F32)

    copies = []
    for d in range(1, npeer):
        peer = lax.rem(me + d, npeer)
        copy = pltpu.make_async_remote_copy(
            parts.at[me], parts.at[me], pool_send.at[d - 1], pool_recv.at[d - 1],
            device_id={"band": peer // nr, "rep": lax.rem(peer, nr)}, device_id_type=MESH,
        )
        copy.start()
        copies.append(copy)
    held = csl[...]
    pre = jnp.dot(u_state[...], held, precision=HIGHEST, preferred_element_type=F32) + coarse_bias
    for copy in copies:
        copy.wait()
    halves = []
    for r in range(nr):
        total = parts[r]
        for b in range(1, nb):
            total = total + parts[b * nr + r]
        halves.append(pltpu.roll(total, lax.rem(slots * cw - band * (own * cw), slots * cw), 1))
    wide = jnp.concatenate(
        [jnp.concatenate([x[i * half : (i + 1) * half] for x in halves], axis=0) for i in range(cr)], axis=1
    )
    pre = pre + jnp.dot(u_pool[...], wide, precision=HIGHEST, preferred_element_type=F32)
    new = held + jnp.tanh(pre)
    for k in range(own):
        for i in range(cr):
            cout[k, :, i, :] = new[:, i * cols + k * cw : i * cols + (k + 1) * cw]


def shards(nt, nb, nr, features, state, live, nbrs, perm, cs, wu, bu, wr, br, wc, bc, u_pool, u_state, b_coarse):
    bands, slots, chans, rows, cols = state.shape
    ins = features.shape[2]
    width = ins + chans
    half = chans // nr
    km = width * rows
    slab = 32
    k1, k2, k3 = 3 * (km + 2 * slab), 3 * (km + 4 * slab), 12 * slab
    cr = rows // 4
    hbm = pl.BlockSpec(memory_space=pl.ANY)
    vm = pl.BlockSpec(memory_space=pltpu.VMEM)
    sm = pl.BlockSpec(memory_space=pltpu.SMEM)
    features = features.reshape(bands, slots, ins * rows, cols)
    state = state.reshape(bands, slots, chans * rows, cols)
    big = (features, state, cs, wu, wr, wc, u_pool, u_state)
    return pl.pallas_call(
        functools.partial(kernel, nt, nb, nr, ins, rows),
        out_shape=(
            jax.ShapeDtypeStruct((bands, slots, half, rows, cols), F32),
            jax.ShapeDtypeStruct(cs.shape, F32),
        ),
        in_specs=[sm] * 7 + [hbm] * len(big),
        out_specs=(vm, vm),
        scratch_shapes=[pltpu.VMEM(x.shape, x.dtype) for x in big]
        + [
            pltpu.VMEM((bands, slots, ins * rows, cols), F32),
            pltpu.VMEM((bands, 3, slab, cols), BF16),
            pltpu.VMEM((bands, 3, slab, cols), BF16),
            pltpu.VMEM((bands, 3, slab, cols), BF16),
            pltpu.VMEM((bands, 3, slab, cols), BF16),
            pltpu.VMEM((slots + 2, bands, slab, cols), BF16),
            pltpu.VMEM((slots + 2, bands, slab, cols), BF16),
            pltpu.VMEM((slots + 2, bands, 2, slab, cols), BF16),
            pltpu.VMEM((slots + 2, bands, 2, slab, cols), BF16),
            pltpu.VMEM((k3, 2 * bands * cols), BF16),
            pltpu.VMEM((slots, bands, (half + chans) * rows, cols), F32),
            pltpu.VMEM((6, chans, k1), F32),
            pltpu.VMEM((3, chans, k2), F32),
            pltpu.VMEM((3, chans, k3), F32),
            pltpu.VMEM(((half + chans) * rows, k1), BF16),
            pltpu.VMEM((half * rows, k2), BF16),
            pltpu.VMEM((2 * chans, k3), BF16),
            pltpu.VMEM((slots, k1, bands * cols), BF16),
            pltpu.VMEM((slots, k2, bands * cols), BF16),
            pltpu.VMEM((nb * nr, cr * half, cols), F32),
            pltpu.VMEM((chans, cr * cols), F32),
            pltpu.SemaphoreType.DMA((len(big),)),
            pltpu.SemaphoreType.DMA((2,)),
            pltpu.SemaphoreType.DMA((2,)),
            pltpu.SemaphoreType.DMA((nb * nr - 1,)),
            pltpu.SemaphoreType.DMA((nb * nr - 1,)),
        ],
        compiler_params=pltpu.CompilerParams(
            collective_id=0, has_side_effects=True, vmem_limit_bytes=56 * 1024 * 1024
        ),
    )(live, nbrs.T, perm, bu, br, bc, b_coarse, *big)


def solution(mesh):
    nt, nb, nr = mesh.shape["tiles"], mesh.shape["band"], mesh.shape["rep"]
    return jax.shard_map(
        functools.partial(shards, nt, nb, nr),
        mesh=mesh,
        in_specs=(
            P(("groups", "band"), "tiles", None, None, None),
            P(("groups", "band"), "tiles", None, None, None),
            P("tiles"),
            P("tiles", None),
            P("tiles", None),
            P(("groups", "tiles", "band"), None, None, None),
            P(),
            P(),
            P(),
            P(),
            P(),
            P(),
            P(),
            P(),
            P(),
        ),
        out_specs=(
            P(("groups", "band"), "tiles", "rep", None, None),
            P(("groups", "tiles", "band"), None, None, None),
        ),
        check_vma=False,
    )
```

```python
import functools

import jax
import jax.numpy as jnp
from jax import lax
from jax.experimental import pallas as pl
from jax.experimental.pallas import tpu as pltpu
from jax.sharding import PartitionSpec as P

MESH = pl.DeviceIdType.MESH
HIGHEST = lax.Precision.HIGHEST
F32 = jnp.float32
BF16 = jnp.bfloat16


def iota(shape, dim):
    return lax.broadcasted_iota(jnp.int32, shape, dim)


def sigmoid(x):
    return 0.5 * jnp.tanh(0.5 * x) + 0.5


def shifted(x, step):
    width = x.shape[1]
    wide = pltpu.roll(x, (-step) % width, 1)
    column = iota(x.shape, 1) + step
    return jnp.where((column >= 0) & (column < width), wide, jnp.zeros_like(wide))


def kernel(
    nt, nb, nr, ins, rows,
    live, nbrs, perm, bu, br, bc, b_coarse, features_in, state_in, cs_in, wu_in, wr_in, wc_in, u_state_in,
    new_out, parts_out, coarse_out,
    features, state, cs, wu, wr, wc, u_state, out, coarse,
    feats, send_up, send_dn, got_up, got_dn, tops, bots, gtops, gbots, strip, gates,
    w1, w2, w3, t1, t2, t3, x1, x2, part,
    load_sems, up_sems, dn_sems, pool_send, pool_recv, store_sems,
):
    bands, slots, flat, cols = state.shape
    chans = flat // rows
    half = chans // nr
    width = ins + chans
    own, cr, cw = cs.shape[0], cs.shape[2], cs.shape[3]
    km = width * rows
    slab = strip.shape[0] // 12
    tile = lax.axis_index("tiles")
    band = lax.axis_index("band")
    rep = lax.axis_index("rep")
    base = tile * slots
    npeer = nb * nr
    me = band * nr + rep
    start = rep * half

    loads = [
        pltpu.make_async_copy(src, dst, load_sems.at[i])
        for i, (src, dst) in enumerate(
            (
                (wu_in, wu), (wr_in, wr), (wc_in, wc), (features_in, features), (state_in, state),
                (cs_in, cs), (u_state_in, u_state),
            )
        )
    ]
    for load in loads:
        load.start()

    barrier = pltpu.get_barrier_semaphore()
    has_up, has_dn = tile > 0, tile < nt - 1

    @pl.when(has_up)
    def _():
        pl.semaphore_signal(barrier, inc=1, device_id={"tiles": tile - 1}, device_id_type=MESH)

    @pl.when(has_dn)
    def _():
        pl.semaphore_signal(barrier, inc=1, device_id={"tiles": tile + 1}, device_id_type=MESH)

    for d in range(1, npeer):
        peer = lax.rem(me + d, npeer)
        pl.semaphore_signal(
            barrier, inc=1, device_id={"band": peer // nr, "rep": lax.rem(peer, nr)}, device_id_type=MESH
        )

    first = jnp.int32(0)
    last = jnp.int32(0)
    for s in range(slots):
        u, d = nbrs[0, s], nbrs[1, s]
        alive = live[s] > 0
        first = jnp.where(alive & ((u < base) | (u >= base + slots)), s, first)
        last = jnp.where(alive & ((d < base) | (d >= base + slots)), s, last)

    def lanes(size, main, halo):
        part = size // 3
        k = iota((1, size), 1)
        side = (k >= part).astype(jnp.int32) + (k >= 2 * part).astype(jnp.int32)
        q = k - part * side
        h = q - main
        chan = jnp.where(h >= 0, h & (slab - 1), q >> 4)
        row = q & (rows - 1)
        for j, at in enumerate(halo):
            row = jnp.where(h >= j * slab, at, row)
        entry = jnp.where(chan < chans, chan + ins, chan - chans)
        return jnp.where(chan < width, entry + 32 * side, -1), row

    def spread(target, weights, main, halo):
        size = target.shape[2]
        entry, _ = lanes(size, main, halo)
        total = jnp.zeros((3 * chans * len(weights), size), F32)
        for b in range(3):
            stack = jnp.concatenate([w[3 * a + b] for w in weights for a in range(3)], axis=0)
            pick = (entry == iota((width, size), 0) + 32 * b).astype(F32).astype(BF16)
            total = total + jnp.dot(stack, pick, preferred_element_type=F32)
        target[...] = total.reshape(target.shape)

    def fill(target, source, jobs, main, halo, dilation):
        shape = (rows, target.shape[1])
        _, row = lanes(shape[1], main, halo)
        delta = row - iota(shape, 0)
        hits = [(delta == a * dilation).astype(F32).astype(BF16) for a in (-1, 0, 1)]
        for at, gate, outs, count in jobs:
            for o in range(count):
                total = None
                for a in range(3):
                    line = jnp.broadcast_to(source[3 * gate + a, pl.ds(outs + o, 1), :], shape).astype(BF16)
                    total = line * hits[a] if total is None else total + line * hits[a]
                target[at + o * rows : at + (o + 1) * rows, :] = total

    mu = half * rows
    halo1, halo2, halo3 = (-1, rows), (-2, -1, rows, rows + 1), (-3, -2, -1, 0)
    for load in loads[:3]:
        load.wait()
    spread(w1, (wu, wr), km, halo1)
    spread(w2, (wc,), km, halo2)
    spread(w3, (wr,), 0, halo3)
    loads[3].wait()
    loads[4].wait()
    for s in range(slots):
        for b in range(bands):
            feats[b, s] = features[b, s].astype(F32)

    blank = jnp.zeros((slab - width, cols), F32)

    def feat_rows(b, s, row):
        return jnp.concatenate([feats[b, s, ch * rows + row : ch * rows + row + 1] for ch in range(ins)] + [blank], axis=0)

    def row_slab(b, s, row):
        return jnp.concatenate([state[b, s, pl.ds(row, chans, stride=rows), :], feat_rows(b, s, row)], axis=0).astype(BF16)

    for b in range(bands):
        for i in range(3):
            send_up[b, i] = row_slab(b, first, i)
            send_dn[b, i] = row_slab(b, last, rows - 3 + i)

    pl.semaphore_wait(barrier, npeer - 1 + jnp.where(has_up, 1, 0) + jnp.where(has_dn, 1, 0))

    def copy_up():
        return pltpu.make_async_remote_copy(
            send_up, got_dn, up_sems.at[0], up_sems.at[1], device_id={"tiles": tile - 1}, device_id_type=MESH
        )

    def copy_dn():
        return pltpu.make_async_remote_copy(
            send_dn, got_up, dn_sems.at[0], dn_sems.at[1], device_id={"tiles": tile + 1}, device_id_type=MESH
        )

    @pl.when(has_up)
    def _():
        copy_up().start()

    @pl.when(has_dn)
    def _():
        copy_dn().start()

    @pl.when(jnp.logical_not(has_up))
    def _():
        got_up[...] = jnp.zeros_like(got_up)

    @pl.when(jnp.logical_not(has_dn))
    def _():
        got_dn[...] = jnp.zeros_like(got_dn)

    fill(t1, w1, ((0, 0, start, half), (mu, 1, 0, chans)), km, halo1, 1)
    fill(t2, w2, ((0, 0, start, half),), km, halo2, 2)
    _, row3 = lanes(t3.shape[1], 0, halo3)
    for i in range(2):
        total = jnp.zeros((chans, t3.shape[1]), F32)
        for a in range(3):
            total = jnp.where(row3 == i - 2 + a - 1, w3[a], total)
        t3[i * chans : (i + 1) * chans] = total.astype(BF16)

    for load in loads[5:]:
        load.wait()
    coarse[0] = jnp.zeros_like(coarse[0])
    for k in range(own):
        for i in range(cr):
            coarse[0, :, i * cols + k * cw : i * cols + (k + 1) * cw] = cs[k, :, i, :]
    coarse_bias = jnp.zeros((chans, 1), F32)
    for o in range(chans):
        coarse_bias = jnp.where(iota((chans, 1), 0) == o, b_coarse[o], coarse_bias)
    coarse[1] = jnp.dot(u_state[...], coarse[0], precision=HIGHEST, preferred_element_type=F32) + coarse_bias
    stores = [pltpu.make_async_copy(coarse, coarse_out, store_sems.at[0])]
    stores[0].start()

    k1, k2 = km + 2 * slab, km + 4 * slab
    for s in range(slots):
        for b in range(bands):
            at = slice(b * cols, (b + 1) * cols)
            tops[s, b] = row_slab(b, s, 0)
            bots[s, b] = row_slab(b, s, rows - 1)
            x = state[b, s].astype(BF16)
            f = features[b, s]
            for j, step in enumerate((-1, 0, 1)):
                x1[s, j * k1 : j * k1 + flat, at] = shifted(x, step) if step else x
                x1[s, j * k1 + flat : j * k1 + km, at] = shifted(f, step) if step else f
                x2[s, j * k2 + flat : j * k2 + km, at] = shifted(f, 2 * step) if step else f
    tops[slots + 1] = jnp.zeros((bands, slab, cols), BF16)
    bots[slots + 1] = jnp.zeros((bands, slab, cols), BF16)
    gtops[slots + 1] = jnp.zeros((bands, 2, slab, cols), BF16)
    gbots[slots + 1] = jnp.zeros((bands, 2, slab, cols), BF16)
    edge_up = [row_slab(b, first, 0) for b in range(bands)]
    edge_dn = [row_slab(b, last, rows - 1) for b in range(bands)]

    @pl.when(has_up)
    def _():
        copy_up().wait_send()

    @pl.when(has_dn)
    def _():
        copy_up().wait_recv()

    @pl.when(has_dn)
    def _():
        copy_dn().wait_send()

    @pl.when(has_up)
    def _():
        copy_dn().wait_recv()

    for b in range(bands):
        bots[slots, b] = got_up[b, 2]
        tops[slots, b] = got_dn[b, 0]

    def place(s, side):
        n = nbrs[side, s]
        here = (n >= base) & (n < base + slots)
        return jnp.where(here, n - base, jnp.where(n >= 0, slots, slots + 1))

    updates = []
    for s in range(slots):
        above, below = place(s, 0), place(s, 1)
        for b in range(bands):
            at = slice(b * cols, (b + 1) * cols)
            x = jnp.concatenate([bots[above, b], tops[below, b]], axis=0)
            for j, step in enumerate((-1, 0, 1)):
                x1[s, j * k1 + km : (j + 1) * k1, at] = shifted(x, step) if step else x
        acc = jnp.dot(t1[...], x1[s], preferred_element_type=F32)
        for b in range(bands):
            at = slice(b * cols, (b + 1) * cols)
            for o in range(half):
                gates[s, b, o * rows : (o + 1) * rows] = sigmoid(acc[o * rows : (o + 1) * rows, at] + bu[start + o])
            for o in range(chans):
                reset = sigmoid(acc[mu + o * rows : mu + (o + 1) * rows, at] + br[o])
                held = state[b, s, o * rows : (o + 1) * rows].astype(BF16).astype(F32)
                gates[s, b, mu + o * rows : mu + (o + 1) * rows] = reset * held
            x = gates[s, b, mu:].astype(BF16)
            for j, step in enumerate((-1, 0, 1)):
                x2[s, j * k2 : j * k2 + flat, at] = shifted(x, 2 * step) if step else x
            for i in range(2):
                for target, row in ((gtops, i), (gbots, rows - 2 + i)):
                    g = gates[s, b, pl.ds(mu + row, chans, stride=rows), :]
                    target[s, b, i] = jnp.concatenate([g, feat_rows(b, s, row)], axis=0).astype(BF16)

    for b in range(bands):
        for side in range(2):
            four = [got_up[b, i] for i in range(3)] + [edge_up[b]] if side == 0 else [edge_dn[b]] + [got_dn[b, i] for i in range(3)]
            at = slice((2 * side + b) * cols, (2 * side + b + 1) * cols)
            x = jnp.concatenate(four, axis=0)
            strip[0 : 4 * slab, at] = shifted(x, -1)
            strip[4 * slab : 8 * slab, at] = x
            strip[8 * slab :, at] = shifted(x, 1)
    acc = jnp.dot(t3[...], strip[...], preferred_element_type=F32)
    reset_bias = jnp.zeros((chans, 1), F32)
    for o in range(chans):
        reset_bias = jnp.where(iota((chans, 1), 0) == o, br[o], reset_bias)
    for b in range(bands):
        for side in range(2):
            at = slice((2 * side + b) * cols, (2 * side + b + 1) * cols)
            for i in range(2):
                held = (got_up[b, 1 + i] if side == 0 else got_dn[b, i]).astype(F32)
                reset = sigmoid(acc[i * chans : (i + 1) * chans, at] + reset_bias)
                joined = jnp.concatenate([reset * held[:chans], held[chans:]], axis=0).astype(BF16)
                if side == 0:
                    gbots[slots, b, i] = joined
                else:
                    gtops[slots, b, i] = joined

    pooled = jnp.zeros((mu, slots * cw), F32)
    for s in range(slots):
        above, below = place(s, 0), place(s, 1)
        for b in range(bands):
            at = slice(b * cols, (b + 1) * cols)
            x = jnp.concatenate([gbots[above, b, 0], gbots[above, b, 1], gtops[below, b, 0], gtops[below, b, 1]], axis=0)
            for j, step in enumerate((-1, 0, 1)):
                x2[s, j * k2 + km : (j + 1) * k2, at] = shifted(x, 2 * step) if step else x
        acc = jnp.dot(t2[...], x2[s], preferred_element_type=F32)
        scale = live[s].astype(F32)
        summed = []
        for o in range(half):
            both = None
            for b in range(bands):
                at = slice(b * cols, (b + 1) * cols)
                update = gates[s, b, o * rows : (o + 1) * rows]
                cand = jnp.tanh(acc[o * rows : (o + 1) * rows, at] + bc[start + o])
                held = state[b, s, pl.ds(pl.multiple_of((start + o) * rows, rows), rows), :]
                new = ((1.0 - update) * held + update * cand) * scale
                out[b, s, o] = new
                both = new if both is None else both + new
            summed.append(both)
        stores.append(pltpu.make_async_copy(out.at[:, s], new_out.at[:, s], store_sems.at[s + 1]))
        stores[-1].start()
        summed = jnp.concatenate(summed, axis=0)
        spot = jnp.int32(0)
        for k in range(slots):
            spot = jnp.where(perm[0, k] == s, k, spot)
        gather = jnp.where(
            iota((cols, slots * cw), 1) == spot * cw + (iota((cols, slots * cw), 0) >> 2), 1.0 / 16.0, 0.0
        )
        pooled = pooled + jnp.dot(summed, gather, precision=HIGHEST, preferred_element_type=F32)

    m, q = iota((cr * half, mu), 0), iota((cr * half, mu), 1)
    rowsum = jnp.where(((m & (half - 1)) == (q >> 4)) & ((m >> (half.bit_length() - 1)) == ((q & (rows - 1)) >> 2)), 1.0, 0.0)
    part[...] = jnp.dot(rowsum, pooled, precision=HIGHEST, preferred_element_type=F32)

    copies = []
    for d in range(1, npeer):
        peer = lax.rem(me + d, npeer)
        copy = pltpu.make_async_remote_copy(
            part, parts_out.at[me], pool_send.at[d - 1], pool_recv.at[d - 1],
            device_id={"band": peer // nr, "rep": lax.rem(peer, nr)}, device_id_type=MESH,
        )
        copy.start()
        copies.append(copy)
    stores.append(pltpu.make_async_copy(part, parts_out.at[me], store_sems.at[slots + 1]))
    stores[-1].start()
    for copy in stores + copies:
        copy.wait()


def finish(
    nb, nr, own, parts_in, coarse_in, u_pool_in, new_in, out, cout, parts, coarse, u_pool, load_sems, store_sems
):
    bands, slots, half = new_in.shape[:3]
    cr, cw = cout.shape[2], cout.shape[3]
    cols = slots * cw
    band = lax.axis_index("band")
    loads = [
        pltpu.make_async_copy(src, dst, load_sems.at[i])
        for i, (src, dst) in enumerate(((parts_in, parts), (coarse_in, coarse), (u_pool_in, u_pool)))
    ]
    for load in loads:
        load.start()
    stores = []
    for b in range(bands):
        for s in range(slots):
            stores.append(pltpu.make_async_copy(new_in.at[b, s], out.at[b, s], store_sems.at[b * slots + s]))
            stores[-1].start()
    for load in loads:
        load.wait()
    halves = []
    for r in range(nr):
        total = parts[r]
        for b in range(1, nb):
            total = total + parts[b * nr + r]
        halves.append(pltpu.roll(total, lax.rem(cols - band * (own * cw), cols), 1))
    wide = jnp.concatenate(
        [jnp.concatenate([x[i * half : (i + 1) * half] for x in halves], axis=0) for i in range(cr)], axis=1
    )
    pre = coarse[1] + jnp.dot(u_pool[...], wide, precision=HIGHEST, preferred_element_type=F32)
    new = coarse[0] + jnp.tanh(pre)
    for k in range(own):
        for i in range(cr):
            cout[k, :, i, :] = new[:, i * cols + k * cw : i * cols + (k + 1) * cw]
    for store in stores:
        store.wait()


def shards(nt, nb, nr, features, state, live, nbrs, perm, cs, wu, bu, wr, br, wc, bc, u_pool, u_state, b_coarse):
    bands, slots, chans, rows, cols = state.shape
    ins = features.shape[2]
    width = ins + chans
    half = chans // nr
    km = width * rows
    slab = 32
    k1, k2, k3 = 3 * (km + 2 * slab), 3 * (km + 4 * slab), 12 * slab
    cr = rows // 4
    hbm = pl.BlockSpec(memory_space=pltpu.HBM)
    vm = pl.BlockSpec(memory_space=pltpu.VMEM)
    sm = pl.BlockSpec(memory_space=pltpu.SMEM)
    features = features.reshape(bands, slots, ins * rows, cols)
    state = state.reshape(bands, slots, chans * rows, cols)
    big = (features, state, cs, wu, wr, wc, u_state)
    fine = jax.ShapeDtypeStruct((bands, slots, half, rows, cols), F32)
    pooled = jax.ShapeDtypeStruct((nb * nr, cr * half, cols), F32)
    coarse = jax.ShapeDtypeStruct((2, chans, cr * cols), F32)
    new, parts, held = pl.pallas_call(
        functools.partial(kernel, nt, nb, nr, ins, rows),
        out_shape=(fine, pooled, coarse),
        in_specs=[sm] * 7 + [hbm] * len(big),
        out_specs=(hbm, hbm, hbm),
        scratch_shapes=[pltpu.VMEM(x.shape, x.dtype) for x in big + (fine, coarse)]
        + [
            pltpu.VMEM((bands, slots, ins * rows, cols), F32),
            pltpu.VMEM((bands, 3, slab, cols), BF16),
            pltpu.VMEM((bands, 3, slab, cols), BF16),
            pltpu.VMEM((bands, 3, slab, cols), BF16),
            pltpu.VMEM((bands, 3, slab, cols), BF16),
            pltpu.VMEM((slots + 2, bands, slab, cols), BF16),
            pltpu.VMEM((slots + 2, bands, slab, cols), BF16),
            pltpu.VMEM((slots + 2, bands, 2, slab, cols), BF16),
            pltpu.VMEM((slots + 2, bands, 2, slab, cols), BF16),
            pltpu.VMEM((k3, 2 * bands * cols), BF16),
            pltpu.VMEM((slots, bands, (half + chans) * rows, cols), F32),
            pltpu.VMEM((6, chans, k1), F32),
            pltpu.VMEM((3, chans, k2), F32),
            pltpu.VMEM((3, chans, k3), F32),
            pltpu.VMEM(((half + chans) * rows, k1), BF16),
            pltpu.VMEM((half * rows, k2), BF16),
            pltpu.VMEM((2 * chans, k3), BF16),
            pltpu.VMEM((slots, k1, bands * cols), BF16),
            pltpu.VMEM((slots, k2, bands * cols), BF16),
            pltpu.VMEM((cr * half, cols), F32),
            pltpu.SemaphoreType.DMA((len(big),)),
            pltpu.SemaphoreType.DMA((2,)),
            pltpu.SemaphoreType.DMA((2,)),
            pltpu.SemaphoreType.DMA((nb * nr - 1,)),
            pltpu.SemaphoreType.DMA((nb * nr - 1,)),
            pltpu.SemaphoreType.DMA((slots + 2,)),
        ],
        compiler_params=pltpu.CompilerParams(
            collective_id=0, has_side_effects=True, vmem_limit_bytes=56 * 1024 * 1024
        ),
    )(live, nbrs.T, perm, bu, br, bc, b_coarse, *big)
    return pl.pallas_call(
        functools.partial(finish, nb, nr, cs.shape[0]),
        out_shape=(fine, jax.ShapeDtypeStruct(cs.shape, F32)),
        in_specs=[hbm] * 4,
        out_specs=(hbm, vm),
        scratch_shapes=[
            pltpu.VMEM(pooled.shape, F32),
            pltpu.VMEM(coarse.shape, F32),
            pltpu.VMEM(u_pool.shape, F32),
            pltpu.SemaphoreType.DMA((3,)),
            pltpu.SemaphoreType.DMA((bands * slots,)),
        ],
        compiler_params=pltpu.CompilerParams(vmem_limit_bytes=56 * 1024 * 1024),
    )(parts, held, u_pool, new)


def solution(mesh):
    nt, nb, nr = mesh.shape["tiles"], mesh.shape["band"], mesh.shape["rep"]
    return jax.shard_map(
        functools.partial(shards, nt, nb, nr),
        mesh=mesh,
        in_specs=(
            P(("groups", "band"), "tiles", None, None, None),
            P(("groups", "band"), "tiles", None, None, None),
            P("tiles"),
            P("tiles", None),
            P("tiles", None),
            P(("groups", "tiles", "band"), None, None, None),
            P(),
            P(),
            P(),
            P(),
            P(),
            P(),
            P(),
            P(),
            P(),
        ),
        out_specs=(
            P(("groups", "band"), "tiles", "rep", None, None),
            P(("groups", "tiles", "band"), None, None, None),
        ),
        check_vma=False,
    )
```

```python
import functools

import jax
import jax.numpy as jnp
from jax import lax
from jax.experimental import pallas as pl
from jax.experimental.pallas import tpu as pltpu
from jax.sharding import PartitionSpec as P

MESH = pl.DeviceIdType.MESH
HIGHEST = lax.Precision.HIGHEST
F32 = jnp.float32
BF16 = jnp.bfloat16


def iota(shape, dim):
    return lax.broadcasted_iota(jnp.int32, shape, dim)


def sigmoid(x):
    return 0.5 * jnp.tanh(0.5 * x) + 0.5


def shifted(x, step):
    width = x.shape[1]
    wide = pltpu.roll(x, (-step) % width, 1)
    column = iota(x.shape, 1) + step
    return jnp.where((column >= 0) & (column < width), wide, jnp.zeros_like(wide))


def kernel(
    nt, nb, nr, ins, rows,
    live, nbrs, perm, bu, br, bc, b_coarse, features_in, state_in, cs_in, wu_in, wr_in, wc_in, u_state_in,
    out, parts, coarse,
    features, state, cs, wu, wr, wc, u_state,
    feats, send_up, send_dn, got_up, got_dn, tops, bots, gtops, gbots, strip, gates,
    w1, w2, w3, t1, t2, t3, x1, x2,
    load_sems, up_sems, dn_sems, pool_send, pool_recv,
):
    bands, slots, flat, cols = state.shape
    chans = flat // rows
    half = chans // nr
    width = ins + chans
    own, cr, cw = cs.shape[0], cs.shape[2], cs.shape[3]
    km = width * rows
    slab = strip.shape[0] // 12
    tile = lax.axis_index("tiles")
    band = lax.axis_index("band")
    rep = lax.axis_index("rep")
    base = tile * slots
    npeer = nb * nr
    me = band * nr + rep
    start = rep * half

    loads = [
        pltpu.make_async_copy(src, dst, load_sems.at[i])
        for i, (src, dst) in enumerate(
            (
                (wu_in, wu), (wr_in, wr), (wc_in, wc), (features_in, features), (state_in, state),
                (cs_in, cs), (u_state_in, u_state),
            )
        )
    ]
    for load in loads:
        load.start()

    barrier = pltpu.get_barrier_semaphore()
    has_up, has_dn = tile > 0, tile < nt - 1

    @pl.when(has_up)
    def _():
        pl.semaphore_signal(barrier, inc=1, device_id={"tiles": tile - 1}, device_id_type=MESH)

    @pl.when(has_dn)
    def _():
        pl.semaphore_signal(barrier, inc=1, device_id={"tiles": tile + 1}, device_id_type=MESH)

    for d in range(1, npeer):
        peer = lax.rem(me + d, npeer)
        pl.semaphore_signal(
            barrier, inc=1, device_id={"band": peer // nr, "rep": lax.rem(peer, nr)}, device_id_type=MESH
        )

    first = jnp.int32(0)
    last = jnp.int32(0)
    for s in range(slots):
        u, d = nbrs[0, s], nbrs[1, s]
        alive = live[s] > 0
        first = jnp.where(alive & ((u < base) | (u >= base + slots)), s, first)
        last = jnp.where(alive & ((d < base) | (d >= base + slots)), s, last)

    def lanes(size, main, halo):
        part = size // 3
        k = iota((1, size), 1)
        side = (k >= part).astype(jnp.int32) + (k >= 2 * part).astype(jnp.int32)
        q = k - part * side
        h = q - main
        chan = jnp.where(h >= 0, h & (slab - 1), q >> 4)
        row = q & (rows - 1)
        for j, at in enumerate(halo):
            row = jnp.where(h >= j * slab, at, row)
        entry = jnp.where(chan < chans, chan + ins, chan - chans)
        return jnp.where(chan < width, entry + 32 * side, -1), row

    def spread(target, weights, main, halo):
        size = target.shape[2]
        entry, _ = lanes(size, main, halo)
        total = jnp.zeros((3 * chans * len(weights), size), F32)
        for b in range(3):
            stack = jnp.concatenate([w[3 * a + b] for w in weights for a in range(3)], axis=0)
            pick = (entry == iota((width, size), 0) + 32 * b).astype(F32).astype(BF16)
            total = total + jnp.dot(stack, pick, preferred_element_type=F32)
        target[...] = total.reshape(target.shape)

    def fill(target, source, jobs, main, halo, dilation):
        shape = (rows, target.shape[1])
        _, row = lanes(shape[1], main, halo)
        delta = row - iota(shape, 0)
        hits = [(delta == a * dilation).astype(F32).astype(BF16) for a in (-1, 0, 1)]
        for at, gate, outs, count in jobs:
            for o in range(count):
                total = None
                for a in range(3):
                    line = jnp.broadcast_to(source[3 * gate + a, pl.ds(outs + o, 1), :], shape).astype(BF16)
                    total = line * hits[a] if total is None else total + line * hits[a]
                target[at + o * rows : at + (o + 1) * rows, :] = total

    mu = half * rows
    halo1, halo2, halo3 = (-1, rows), (-2, -1, rows, rows + 1), (-3, -2, -1, 0)
    for load in loads[:3]:
        load.wait()
    spread(w1, (wu, wr), km, halo1)
    spread(w2, (wc,), km, halo2)
    spread(w3, (wr,), 0, halo3)
    loads[3].wait()
    loads[4].wait()
    for s in range(slots):
        for b in range(bands):
            feats[b, s] = features[b, s].astype(F32)

    blank = jnp.zeros((slab - width, cols), F32)

    def feat_rows(b, s, row):
        return jnp.concatenate([feats[b, s, ch * rows + row : ch * rows + row + 1] for ch in range(ins)] + [blank], axis=0)

    def row_slab(b, s, row):
        return jnp.concatenate([state[b, s, pl.ds(row, chans, stride=rows), :], feat_rows(b, s, row)], axis=0).astype(BF16)

    for b in range(bands):
        for i in range(3):
            send_up[b, i] = row_slab(b, first, i)
            send_dn[b, i] = row_slab(b, last, rows - 3 + i)

    pl.semaphore_wait(barrier, npeer - 1 + jnp.where(has_up, 1, 0) + jnp.where(has_dn, 1, 0))

    def copy_up():
        return pltpu.make_async_remote_copy(
            send_up, got_dn, up_sems.at[0], up_sems.at[1], device_id={"tiles": tile - 1}, device_id_type=MESH
        )

    def copy_dn():
        return pltpu.make_async_remote_copy(
            send_dn, got_up, dn_sems.at[0], dn_sems.at[1], device_id={"tiles": tile + 1}, device_id_type=MESH
        )

    @pl.when(has_up)
    def _():
        copy_up().start()

    @pl.when(has_dn)
    def _():
        copy_dn().start()

    @pl.when(jnp.logical_not(has_up))
    def _():
        got_up[...] = jnp.zeros_like(got_up)

    @pl.when(jnp.logical_not(has_dn))
    def _():
        got_dn[...] = jnp.zeros_like(got_dn)

    fill(t1, w1, ((0, 0, start, half), (mu, 1, 0, chans)), km, halo1, 1)
    fill(t2, w2, ((0, 0, start, half),), km, halo2, 2)
    _, row3 = lanes(t3.shape[1], 0, halo3)
    for i in range(2):
        total = jnp.zeros((chans, t3.shape[1]), F32)
        for a in range(3):
            total = jnp.where(row3 == i - 2 + a - 1, w3[a], total)
        t3[i * chans : (i + 1) * chans] = total.astype(BF16)

    for load in loads[5:]:
        load.wait()
    coarse[0] = jnp.zeros_like(coarse[0])
    for k in range(own):
        for i in range(cr):
            coarse[0, :, i * cols + k * cw : i * cols + (k + 1) * cw] = cs[k, :, i, :]
    coarse_bias = jnp.zeros((chans, 1), F32)
    for o in range(chans):
        coarse_bias = jnp.where(iota((chans, 1), 0) == o, b_coarse[o], coarse_bias)
    coarse[1] = jnp.dot(u_state[...], coarse[0], precision=HIGHEST, preferred_element_type=F32) + coarse_bias

    k1, k2 = km + 2 * slab, km + 4 * slab
    for s in range(slots):
        for b in range(bands):
            at = slice(b * cols, (b + 1) * cols)
            tops[s, b] = row_slab(b, s, 0)
            bots[s, b] = row_slab(b, s, rows - 1)
            x = state[b, s].astype(BF16)
            f = features[b, s]
            for j, step in enumerate((-1, 0, 1)):
                x1[s, j * k1 : j * k1 + flat, at] = shifted(x, step) if step else x
                x1[s, j * k1 + flat : j * k1 + km, at] = shifted(f, step) if step else f
                x2[s, j * k2 + flat : j * k2 + km, at] = shifted(f, 2 * step) if step else f
    tops[slots + 1] = jnp.zeros((bands, slab, cols), BF16)
    bots[slots + 1] = jnp.zeros((bands, slab, cols), BF16)
    gtops[slots + 1] = jnp.zeros((bands, 2, slab, cols), BF16)
    gbots[slots + 1] = jnp.zeros((bands, 2, slab, cols), BF16)
    edge_up = [row_slab(b, first, 0) for b in range(bands)]
    edge_dn = [row_slab(b, last, rows - 1) for b in range(bands)]

    @pl.when(has_up)
    def _():
        copy_up().wait_send()

    @pl.when(has_dn)
    def _():
        copy_up().wait_recv()

    @pl.when(has_dn)
    def _():
        copy_dn().wait_send()

    @pl.when(has_up)
    def _():
        copy_dn().wait_recv()

    for b in range(bands):
        bots[slots, b] = got_up[b, 2]
        tops[slots, b] = got_dn[b, 0]

    def place(s, side):
        n = nbrs[side, s]
        here = (n >= base) & (n < base + slots)
        return jnp.where(here, n - base, jnp.where(n >= 0, slots, slots + 1))

    updates = []
    for s in range(slots):
        above, below = place(s, 0), place(s, 1)
        for b in range(bands):
            at = slice(b * cols, (b + 1) * cols)
            x = jnp.concatenate([bots[above, b], tops[below, b]], axis=0)
            for j, step in enumerate((-1, 0, 1)):
                x1[s, j * k1 + km : (j + 1) * k1, at] = shifted(x, step) if step else x
        acc = jnp.dot(t1[...], x1[s], preferred_element_type=F32)
        for b in range(bands):
            at = slice(b * cols, (b + 1) * cols)
            for o in range(half):
                gates[s, b, o * rows : (o + 1) * rows] = sigmoid(acc[o * rows : (o + 1) * rows, at] + bu[start + o])
            for o in range(chans):
                reset = sigmoid(acc[mu + o * rows : mu + (o + 1) * rows, at] + br[o])
                held = state[b, s, o * rows : (o + 1) * rows].astype(BF16).astype(F32)
                gates[s, b, mu + o * rows : mu + (o + 1) * rows] = reset * held
            x = gates[s, b, mu:].astype(BF16)
            for j, step in enumerate((-1, 0, 1)):
                x2[s, j * k2 : j * k2 + flat, at] = shifted(x, 2 * step) if step else x
            for i in range(2):
                for target, row in ((gtops, i), (gbots, rows - 2 + i)):
                    g = gates[s, b, pl.ds(mu + row, chans, stride=rows), :]
                    target[s, b, i] = jnp.concatenate([g, feat_rows(b, s, row)], axis=0).astype(BF16)

    for b in range(bands):
        for side in range(2):
            four = [got_up[b, i] for i in range(3)] + [edge_up[b]] if side == 0 else [edge_dn[b]] + [got_dn[b, i] for i in range(3)]
            at = slice((2 * side + b) * cols, (2 * side + b + 1) * cols)
            x = jnp.concatenate(four, axis=0)
            strip[0 : 4 * slab, at] = shifted(x, -1)
            strip[4 * slab : 8 * slab, at] = x
            strip[8 * slab :, at] = shifted(x, 1)
    acc = jnp.dot(t3[...], strip[...], preferred_element_type=F32)
    reset_bias = jnp.zeros((chans, 1), F32)
    for o in range(chans):
        reset_bias = jnp.where(iota((chans, 1), 0) == o, br[o], reset_bias)
    for b in range(bands):
        for side in range(2):
            at = slice((2 * side + b) * cols, (2 * side + b + 1) * cols)
            for i in range(2):
                held = (got_up[b, 1 + i] if side == 0 else got_dn[b, i]).astype(F32)
                reset = sigmoid(acc[i * chans : (i + 1) * chans, at] + reset_bias)
                joined = jnp.concatenate([reset * held[:chans], held[chans:]], axis=0).astype(BF16)
                if side == 0:
                    gbots[slots, b, i] = joined
                else:
                    gtops[slots, b, i] = joined

    pooled = jnp.zeros((mu, slots * cw), F32)
    for s in range(slots):
        above, below = place(s, 0), place(s, 1)
        for b in range(bands):
            at = slice(b * cols, (b + 1) * cols)
            x = jnp.concatenate([gbots[above, b, 0], gbots[above, b, 1], gtops[below, b, 0], gtops[below, b, 1]], axis=0)
            for j, step in enumerate((-1, 0, 1)):
                x2[s, j * k2 + km : (j + 1) * k2, at] = shifted(x, 2 * step) if step else x
        acc = jnp.dot(t2[...], x2[s], preferred_element_type=F32)
        scale = live[s].astype(F32)
        summed = []
        for o in range(half):
            both = None
            for b in range(bands):
                at = slice(b * cols, (b + 1) * cols)
                update = gates[s, b, o * rows : (o + 1) * rows]
                cand = jnp.tanh(acc[o * rows : (o + 1) * rows, at] + bc[start + o])
                held = state[b, s, pl.ds(pl.multiple_of((start + o) * rows, rows), rows), :]
                new = ((1.0 - update) * held + update * cand) * scale
                out[b, s, o] = new
                both = new if both is None else both + new
            summed.append(both)
        summed = jnp.concatenate(summed, axis=0)
        spot = jnp.int32(0)
        for k in range(slots):
            spot = jnp.where(perm[0, k] == s, k, spot)
        gather = jnp.where(
            iota((cols, slots * cw), 1) == spot * cw + (iota((cols, slots * cw), 0) >> 2), 1.0 / 16.0, 0.0
        )
        pooled = pooled + jnp.dot(summed, gather, precision=HIGHEST, preferred_element_type=F32)

    m, q = iota((cr * half, mu), 0), iota((cr * half, mu), 1)
    rowsum = jnp.where(((m & (half - 1)) == (q >> 4)) & ((m >> (half.bit_length() - 1)) == ((q & (rows - 1)) >> 2)), 1.0, 0.0)
    parts[me] = jnp.dot(rowsum, pooled, precision=HIGHEST, preferred_element_type=F32)

    copies = []
    for d in range(1, npeer):
        peer = lax.rem(me + d, npeer)
        copy = pltpu.make_async_remote_copy(
            parts.at[me], parts.at[me], pool_send.at[d - 1], pool_recv.at[d - 1],
            device_id={"band": peer // nr, "rep": lax.rem(peer, nr)}, device_id_type=MESH,
        )
        copy.start()
        copies.append(copy)
    for copy in copies:
        copy.wait()


def finish(
    nb, nr, own, parts, coarse, u_pool, new_in, out, coarse_out, cout, store_sems
):
    bands, slots, half = new_in.shape[:3]
    cr, cw = cout.shape[2], cout.shape[3]
    cols = slots * cw
    band = lax.axis_index("band")
    stores = []
    for b in range(bands):
        for s in range(slots):
            stores.append(pltpu.make_async_copy(new_in.at[b, s], out.at[b, s], store_sems.at[b * slots + s]))
            stores[-1].start()
    halves = []
    for r in range(nr):
        total = parts[r]
        for b in range(1, nb):
            total = total + parts[b * nr + r]
        halves.append(pltpu.roll(total, lax.rem(cols - band * (own * cw), cols), 1))
    wide = jnp.concatenate(
        [jnp.concatenate([x[i * half : (i + 1) * half] for x in halves], axis=0) for i in range(cr)], axis=1
    )
    pre = coarse[1] + jnp.dot(u_pool[...], wide, precision=HIGHEST, preferred_element_type=F32)
    new = coarse[0] + jnp.tanh(pre)
    for k in range(own):
        for i in range(cr):
            cout[k, :, i, :] = new[:, i * cols + k * cw : i * cols + (k + 1) * cw]
    stores.append(pltpu.make_async_copy(cout, coarse_out, store_sems.at[bands * slots]))
    stores[-1].start()
    for store in stores:
        store.wait()


def shards(nt, nb, nr, features, state, live, nbrs, perm, cs, wu, bu, wr, br, wc, bc, u_pool, u_state, b_coarse):
    bands, slots, chans, rows, cols = state.shape
    ins = features.shape[2]
    width = ins + chans
    half = chans // nr
    km = width * rows
    slab = 32
    k1, k2, k3 = 3 * (km + 2 * slab), 3 * (km + 4 * slab), 12 * slab
    cr = rows // 4
    hbm = pl.BlockSpec(memory_space=pltpu.HBM)
    vm = pl.BlockSpec(memory_space=pltpu.VMEM)
    sm = pl.BlockSpec(memory_space=pltpu.SMEM)
    features = features.reshape(bands, slots, ins * rows, cols)
    state = state.reshape(bands, slots, chans * rows, cols)
    big = tuple(
        pltpu.with_memory_space_constraint(x, pltpu.HBM) for x in (features, state, cs, wu, wr, wc, u_state)
    )
    small = tuple(
        pltpu.with_memory_space_constraint(x, pltpu.HBM) for x in (live, nbrs.T, perm, bu, br, bc, b_coarse)
    )
    fine = jax.ShapeDtypeStruct((bands, slots, half, rows, cols), F32)
    pooled = jax.ShapeDtypeStruct((nb * nr, cr * half, cols), F32)
    coarse = jax.ShapeDtypeStruct((2, chans, cr * cols), F32)
    new, parts, held = pl.pallas_call(
        functools.partial(kernel, nt, nb, nr, ins, rows),
        out_shape=(fine, pooled, coarse),
        in_specs=[sm] * 7 + [hbm] * len(big),
        out_specs=(vm, vm, vm),
        scratch_shapes=[pltpu.VMEM(x.shape, x.dtype) for x in big]
        + [
            pltpu.VMEM((bands, slots, ins * rows, cols), F32),
            pltpu.VMEM((bands, 3, slab, cols), BF16),
            pltpu.VMEM((bands, 3, slab, cols), BF16),
            pltpu.VMEM((bands, 3, slab, cols), BF16),
            pltpu.VMEM((bands, 3, slab, cols), BF16),
            pltpu.VMEM((slots + 2, bands, slab, cols), BF16),
            pltpu.VMEM((slots + 2, bands, slab, cols), BF16),
            pltpu.VMEM((slots + 2, bands, 2, slab, cols), BF16),
            pltpu.VMEM((slots + 2, bands, 2, slab, cols), BF16),
            pltpu.VMEM((k3, 2 * bands * cols), BF16),
            pltpu.VMEM((slots, bands, (half + chans) * rows, cols), F32),
            pltpu.VMEM((6, chans, k1), F32),
            pltpu.VMEM((3, chans, k2), F32),
            pltpu.VMEM((3, chans, k3), F32),
            pltpu.VMEM(((half + chans) * rows, k1), BF16),
            pltpu.VMEM((half * rows, k2), BF16),
            pltpu.VMEM((2 * chans, k3), BF16),
            pltpu.VMEM((slots, k1, bands * cols), BF16),
            pltpu.VMEM((slots, k2, bands * cols), BF16),
            pltpu.SemaphoreType.DMA((len(big),)),
            pltpu.SemaphoreType.DMA((2,)),
            pltpu.SemaphoreType.DMA((2,)),
            pltpu.SemaphoreType.DMA((nb * nr - 1,)),
            pltpu.SemaphoreType.DMA((nb * nr - 1,)),
        ],
        compiler_params=pltpu.CompilerParams(
            collective_id=0, has_side_effects=True, vmem_limit_bytes=24 * 1024 * 1024
        ),
    )(*small, *big)
    return pl.pallas_call(
        functools.partial(finish, nb, nr, cs.shape[0]),
        out_shape=(fine, jax.ShapeDtypeStruct(cs.shape, F32)),
        in_specs=[vm, vm, vm, pl.BlockSpec(memory_space=pl.ANY)],
        out_specs=(hbm, hbm),
        scratch_shapes=[
            pltpu.VMEM(cs.shape, F32),
            pltpu.SemaphoreType.DMA((bands * slots + 1,)),
        ],
        compiler_params=pltpu.CompilerParams(vmem_limit_bytes=24 * 1024 * 1024),
    )(parts, held, u_pool, new)


def solution(mesh):
    nt, nb, nr = mesh.shape["tiles"], mesh.shape["band"], mesh.shape["rep"]
    return jax.shard_map(
        functools.partial(shards, nt, nb, nr),
        mesh=mesh,
        in_specs=(
            P(("groups", "band"), "tiles", None, None, None),
            P(("groups", "band"), "tiles", None, None, None),
            P("tiles"),
            P("tiles", None),
            P("tiles", None),
            P(("groups", "tiles", "band"), None, None, None),
            P(),
            P(),
            P(),
            P(),
            P(),
            P(),
            P(),
            P(),
            P(),
        ),
        out_specs=(
            P(("groups", "band"), "tiles", "rep", None, None),
            P(("groups", "tiles", "band"), None, None, None),
        ),
        check_vma=False,
    )
```

```python
import functools

import jax
import jax.numpy as jnp
from jax import lax
from jax.experimental import pallas as pl
from jax.experimental.pallas import tpu as pltpu
from jax.sharding import PartitionSpec as P

MESH = pl.DeviceIdType.MESH
HIGHEST = lax.Precision.HIGHEST
F32 = jnp.float32
BF16 = jnp.bfloat16


def iota(shape, dim):
    return lax.broadcasted_iota(jnp.int32, shape, dim)


def sigmoid(x):
    return 0.5 * jnp.tanh(0.5 * x) + 0.5


def thirds(x):
    high = x.astype(BF16)
    rest = x - high.astype(F32)
    middle = rest.astype(BF16)
    return high, middle, (rest - middle.astype(F32)).astype(BF16)


def shifted(x, step):
    width = x.shape[1]
    wide = pltpu.roll(x, (-step) % width, 1)
    column = iota(x.shape, 1) + step
    return jnp.where((column >= 0) & (column < width), wide, jnp.zeros_like(wide))


def kernel(
    nt, nb, nr, ins, rows,
    live_in, nbrs_in, perm_in, bu_in, br_in, bc_in, b_coarse_in, features_in, state_in, cs_in, wu_in, wr_in, wc_in, u_state_in,
    out, parts, coarse,
    live, nbrs, perm, bu, br, bc, b_coarse, features, state, cs, wu, wr, wc, u_state,
    feats, send_up, send_dn, got_up, got_dn, tops, bots, gtops, gbots, strip, gates,
    w1, w2, w3, t1, t2, t3, x1, x2,
    load_sems, up_sems, dn_sems, pool_send, pool_recv,
):
    bands, slots, flat, cols = state.shape
    chans = flat // rows
    half = chans // nr
    width = ins + chans
    own, cr, cw = cs.shape[0], cs.shape[2], cs.shape[3]
    km = width * rows
    slab = strip.shape[0] // 12
    tile = lax.axis_index("tiles")
    band = lax.axis_index("band")
    rep = lax.axis_index("rep")
    base = tile * slots
    npeer = nb * nr
    me = band * nr + rep
    start = rep * half

    loads = [
        pltpu.make_async_copy(src, dst, load_sems.at[i])
        for i, (src, dst) in enumerate(
            (
                (wu_in, wu), (wr_in, wr), (wc_in, wc), (features_in, features), (state_in, state),
                (cs_in, cs), (u_state_in, u_state),
                (live_in, live), (nbrs_in, nbrs), (perm_in, perm),
                (bu_in, bu), (br_in, br), (bc_in, bc), (b_coarse_in, b_coarse),
            )
        )
    ]
    for load in loads:
        load.start()

    barrier = pltpu.get_barrier_semaphore()
    has_up, has_dn = tile > 0, tile < nt - 1

    @pl.when(has_up)
    def _():
        pl.semaphore_signal(barrier, inc=1, device_id={"tiles": tile - 1}, device_id_type=MESH)

    @pl.when(has_dn)
    def _():
        pl.semaphore_signal(barrier, inc=1, device_id={"tiles": tile + 1}, device_id_type=MESH)

    for d in range(1, npeer):
        peer = lax.rem(me + d, npeer)
        pl.semaphore_signal(
            barrier, inc=1, device_id={"band": peer // nr, "rep": lax.rem(peer, nr)}, device_id_type=MESH
        )

    def lanes(size, main, halo):
        part = size // 3
        k = iota((1, size), 1)
        side = (k >= part).astype(jnp.int32) + (k >= 2 * part).astype(jnp.int32)
        q = k - part * side
        h = q - main
        chan = jnp.where(h >= 0, h & (slab - 1), q >> 4)
        row = q & (rows - 1)
        for j, at in enumerate(halo):
            row = jnp.where(h >= j * slab, at, row)
        entry = jnp.where(chan < chans, chan + ins, chan - chans)
        return jnp.where(chan < width, entry + 32 * side, -1), row

    def spread(target, weights, main, halo):
        size = target.shape[2]
        entry, _ = lanes(size, main, halo)
        total = jnp.zeros((3 * chans * len(weights), size), F32)
        for b in range(3):
            stack = jnp.concatenate([w[3 * a + b] for w in weights for a in range(3)], axis=0)
            pick = (entry == iota((width, size), 0) + 32 * b).astype(F32).astype(BF16)
            total = total + jnp.dot(stack, pick, preferred_element_type=F32)
        target[...] = total.reshape(target.shape)

    def fill(target, source, jobs, main, halo, dilation):
        shape = (rows, target.shape[1])
        _, row = lanes(shape[1], main, halo)
        delta = row - iota(shape, 0)
        hits = [(delta == a * dilation).astype(F32).astype(BF16) for a in (-1, 0, 1)]
        for at, gate, outs, count in jobs:
            for o in range(count):
                total = None
                for a in range(3):
                    line = jnp.broadcast_to(source[3 * gate + a, pl.ds(outs + o, 1), :], shape).astype(BF16)
                    total = line * hits[a] if total is None else total + line * hits[a]
                target[at + o * rows : at + (o + 1) * rows, :] = total

    mu = half * rows
    halo1, halo2, halo3 = (-1, rows), (-2, -1, rows, rows + 1), (-3, -2, -1, 0)
    for load in loads[:3]:
        load.wait()
    spread(w1, (wu, wr), km, halo1)
    spread(w2, (wc,), km, halo2)
    spread(w3, (wr,), 0, halo3)
    for load in loads[7:]:
        load.wait()
    first = jnp.int32(0)
    last = jnp.int32(0)
    for s in range(slots):
        u, d = nbrs[0, s], nbrs[1, s]
        alive = live[s] > 0
        first = jnp.where(alive & ((u < base) | (u >= base + slots)), s, first)
        last = jnp.where(alive & ((d < base) | (d >= base + slots)), s, last)

    loads[3].wait()
    loads[4].wait()
    for s in range(slots):
        for b in range(bands):
            feats[b, s] = features[b, s].astype(F32)

    blank = jnp.zeros((slab - width, cols), F32)

    def feat_rows(b, s, row):
        return jnp.concatenate([feats[b, s, ch * rows + row : ch * rows + row + 1] for ch in range(ins)] + [blank], axis=0)

    def row_slab(b, s, row):
        return jnp.concatenate([state[b, s, pl.ds(row, chans, stride=rows), :], feat_rows(b, s, row)], axis=0).astype(BF16)

    for b in range(bands):
        for i in range(3):
            send_up[b, i] = row_slab(b, first, i)
            send_dn[b, i] = row_slab(b, last, rows - 3 + i)

    pl.semaphore_wait(barrier, npeer - 1 + jnp.where(has_up, 1, 0) + jnp.where(has_dn, 1, 0))

    def copy_up():
        return pltpu.make_async_remote_copy(
            send_up, got_dn, up_sems.at[0], up_sems.at[1], device_id={"tiles": tile - 1}, device_id_type=MESH
        )

    def copy_dn():
        return pltpu.make_async_remote_copy(
            send_dn, got_up, dn_sems.at[0], dn_sems.at[1], device_id={"tiles": tile + 1}, device_id_type=MESH
        )

    @pl.when(has_up)
    def _():
        copy_up().start()

    @pl.when(has_dn)
    def _():
        copy_dn().start()

    @pl.when(jnp.logical_not(has_up))
    def _():
        got_up[...] = jnp.zeros_like(got_up)

    @pl.when(jnp.logical_not(has_dn))
    def _():
        got_dn[...] = jnp.zeros_like(got_dn)

    fill(t1, w1, ((0, 0, start, half), (mu, 1, 0, chans)), km, halo1, 1)
    fill(t2, w2, ((0, 0, start, half),), km, halo2, 2)
    _, row3 = lanes(t3.shape[1], 0, halo3)
    for i in range(2):
        total = jnp.zeros((chans, t3.shape[1]), F32)
        for a in range(3):
            total = jnp.where(row3 == i - 2 + a - 1, w3[a], total)
        t3[i * chans : (i + 1) * chans] = total.astype(BF16)

    for load in loads[5:7]:
        load.wait()
    coarse[0] = jnp.zeros_like(coarse[0])
    for k in range(own):
        for i in range(cr):
            coarse[0, :, i * cols + k * cw : i * cols + (k + 1) * cw] = cs[k, :, i, :]
    coarse_bias = jnp.zeros((chans, 1), F32)
    for o in range(chans):
        coarse_bias = jnp.where(iota((chans, 1), 0) == o, b_coarse[o], coarse_bias)
    coarse[1] = jnp.dot(u_state[...], coarse[0], precision=HIGHEST, preferred_element_type=F32) + coarse_bias

    k1, k2 = km + 2 * slab, km + 4 * slab
    for s in range(slots):
        for b in range(bands):
            at = slice(b * cols, (b + 1) * cols)
            tops[s, b] = row_slab(b, s, 0)
            bots[s, b] = row_slab(b, s, rows - 1)
            x = state[b, s].astype(BF16)
            f = features[b, s]
            for j, step in enumerate((-1, 0, 1)):
                x1[s, j * k1 : j * k1 + flat, at] = shifted(x, step) if step else x
                x1[s, j * k1 + flat : j * k1 + km, at] = shifted(f, step) if step else f
                x2[s, j * k2 + flat : j * k2 + km, at] = shifted(f, 2 * step) if step else f
    tops[slots + 1] = jnp.zeros((bands, slab, cols), BF16)
    bots[slots + 1] = jnp.zeros((bands, slab, cols), BF16)
    gtops[slots + 1] = jnp.zeros((bands, 2, slab, cols), BF16)
    gbots[slots + 1] = jnp.zeros((bands, 2, slab, cols), BF16)
    edge_up = [row_slab(b, first, 0) for b in range(bands)]
    edge_dn = [row_slab(b, last, rows - 1) for b in range(bands)]

    @pl.when(has_up)
    def _():
        copy_up().wait_send()

    @pl.when(has_dn)
    def _():
        copy_up().wait_recv()

    @pl.when(has_dn)
    def _():
        copy_dn().wait_send()

    @pl.when(has_up)
    def _():
        copy_dn().wait_recv()

    for b in range(bands):
        bots[slots, b] = got_up[b, 2]
        tops[slots, b] = got_dn[b, 0]

    def place(s, side):
        n = nbrs[side, s]
        here = (n >= base) & (n < base + slots)
        return jnp.where(here, n - base, jnp.where(n >= 0, slots, slots + 1))

    updates = []
    for s in range(slots):
        above, below = place(s, 0), place(s, 1)
        for b in range(bands):
            at = slice(b * cols, (b + 1) * cols)
            x = jnp.concatenate([bots[above, b], tops[below, b]], axis=0)
            for j, step in enumerate((-1, 0, 1)):
                x1[s, j * k1 + km : (j + 1) * k1, at] = shifted(x, step) if step else x
        acc = jnp.dot(t1[...], x1[s], preferred_element_type=F32)
        for b in range(bands):
            at = slice(b * cols, (b + 1) * cols)
            for o in range(half):
                gates[s, b, o * rows : (o + 1) * rows] = sigmoid(acc[o * rows : (o + 1) * rows, at] + bu[start + o])
            for o in range(chans):
                reset = sigmoid(acc[mu + o * rows : mu + (o + 1) * rows, at] + br[o])
                held = state[b, s, o * rows : (o + 1) * rows].astype(BF16).astype(F32)
                gates[s, b, mu + o * rows : mu + (o + 1) * rows] = reset * held
            x = gates[s, b, mu:].astype(BF16)
            for j, step in enumerate((-1, 0, 1)):
                x2[s, j * k2 : j * k2 + flat, at] = shifted(x, 2 * step) if step else x
            for i in range(2):
                for target, row in ((gtops, i), (gbots, rows - 2 + i)):
                    g = gates[s, b, pl.ds(mu + row, chans, stride=rows), :]
                    target[s, b, i] = jnp.concatenate([g, feat_rows(b, s, row)], axis=0).astype(BF16)

    for b in range(bands):
        for side in range(2):
            four = [got_up[b, i] for i in range(3)] + [edge_up[b]] if side == 0 else [edge_dn[b]] + [got_dn[b, i] for i in range(3)]
            at = slice((2 * side + b) * cols, (2 * side + b + 1) * cols)
            x = jnp.concatenate(four, axis=0)
            strip[0 : 4 * slab, at] = shifted(x, -1)
            strip[4 * slab : 8 * slab, at] = x
            strip[8 * slab :, at] = shifted(x, 1)
    acc = jnp.dot(t3[...], strip[...], preferred_element_type=F32)
    reset_bias = jnp.zeros((chans, 1), F32)
    for o in range(chans):
        reset_bias = jnp.where(iota((chans, 1), 0) == o, br[o], reset_bias)
    for b in range(bands):
        for side in range(2):
            at = slice((2 * side + b) * cols, (2 * side + b + 1) * cols)
            for i in range(2):
                held = (got_up[b, 1 + i] if side == 0 else got_dn[b, i]).astype(F32)
                reset = sigmoid(acc[i * chans : (i + 1) * chans, at] + reset_bias)
                joined = jnp.concatenate([reset * held[:chans], held[chans:]], axis=0).astype(BF16)
                if side == 0:
                    gbots[slots, b, i] = joined
                else:
                    gtops[slots, b, i] = joined

    pooled = jnp.zeros((mu, slots * cw), F32)
    for s in range(slots):
        above, below = place(s, 0), place(s, 1)
        for b in range(bands):
            at = slice(b * cols, (b + 1) * cols)
            x = jnp.concatenate([gbots[above, b, 0], gbots[above, b, 1], gtops[below, b, 0], gtops[below, b, 1]], axis=0)
            for j, step in enumerate((-1, 0, 1)):
                x2[s, j * k2 + km : (j + 1) * k2, at] = shifted(x, 2 * step) if step else x
        acc = jnp.dot(t2[...], x2[s], preferred_element_type=F32)
        scale = live[s].astype(F32)
        summed = []
        for o in range(half):
            both = None
            for b in range(bands):
                at = slice(b * cols, (b + 1) * cols)
                update = gates[s, b, o * rows : (o + 1) * rows]
                cand = jnp.tanh(acc[o * rows : (o + 1) * rows, at] + bc[start + o])
                held = state[b, s, pl.ds(pl.multiple_of((start + o) * rows, rows), rows), :]
                new = ((1.0 - update) * held + update * cand) * scale
                out[b, s, o] = new
                both = new if both is None else both + new
            summed.append(both)
        summed = jnp.concatenate(summed, axis=0)
        spot = jnp.int32(0)
        for k in range(slots):
            spot = jnp.where(perm[0, k] == s, k, spot)
        gather = jnp.where(
            iota((cols, slots * cw), 1) == spot * cw + (iota((cols, slots * cw), 0) >> 2), 1.0 / 16.0, 0.0
        )
        product = jnp.dot(jnp.concatenate(thirds(summed), axis=0), gather.astype(BF16), preferred_element_type=F32)
        pooled = pooled + (product[:mu] + (product[mu : 2 * mu] + product[2 * mu :]))

    m, q = iota((cr * half, mu), 0), iota((cr * half, mu), 1)
    rowsum = jnp.where(((m & (half - 1)) == (q >> 4)) & ((m >> (half.bit_length() - 1)) == ((q & (rows - 1)) >> 2)), 1.0, 0.0)
    product = jnp.dot(rowsum.astype(BF16), jnp.concatenate(thirds(pooled), axis=1), preferred_element_type=F32)
    parts[me] = product[:, :cols] + (product[:, cols : 2 * cols] + product[:, 2 * cols :])

    copies = []
    for d in range(1, npeer):
        peer = lax.rem(me + d, npeer)
        copy = pltpu.make_async_remote_copy(
            parts.at[me], parts.at[me], pool_send.at[d - 1], pool_recv.at[d - 1],
            device_id={"band": peer // nr, "rep": lax.rem(peer, nr)}, device_id_type=MESH,
        )
        copy.start()
        copies.append(copy)
    for copy in copies:
        copy.wait()


def finish(
    nb, nr, own, parts, coarse, u_pool, new_in, out, coarse_out, cout, store_sems
):
    bands, slots, half = new_in.shape[:3]
    cr, cw = cout.shape[2], cout.shape[3]
    cols = slots * cw
    band = lax.axis_index("band")
    stores = []
    for b in range(bands):
        for s in range(slots):
            stores.append(pltpu.make_async_copy(new_in.at[b, s], out.at[b, s], store_sems.at[b * slots + s]))
            stores[-1].start()
    halves = []
    for r in range(nr):
        total = parts[r]
        for b in range(1, nb):
            total = total + parts[b * nr + r]
        halves.append(pltpu.roll(total, lax.rem(cols - band * (own * cw), cols), 1))
    wide = jnp.concatenate(
        [jnp.concatenate([x[i * half : (i + 1) * half] for x in halves], axis=0) for i in range(cr)], axis=1
    )
    pre = coarse[1] + jnp.dot(u_pool[...], wide, precision=HIGHEST, preferred_element_type=F32)
    new = coarse[0] + jnp.tanh(pre)
    for k in range(own):
        for i in range(cr):
            cout[k, :, i, :] = new[:, i * cols + k * cw : i * cols + (k + 1) * cw]
    stores.append(pltpu.make_async_copy(cout, coarse_out, store_sems.at[bands * slots]))
    stores[-1].start()
    for store in stores:
        store.wait()


def shards(nt, nb, nr, features, state, live, nbrs, perm, cs, wu, bu, wr, br, wc, bc, u_pool, u_state, b_coarse):
    bands, slots, chans, rows, cols = state.shape
    ins = features.shape[2]
    width = ins + chans
    half = chans // nr
    km = width * rows
    slab = 32
    k1, k2, k3 = 3 * (km + 2 * slab), 3 * (km + 4 * slab), 12 * slab
    cr = rows // 4
    hbm = pl.BlockSpec(memory_space=pltpu.HBM)
    vm = pl.BlockSpec(memory_space=pltpu.VMEM)
    features = features.reshape(bands, slots, ins * rows, cols)
    state = state.reshape(bands, slots, chans * rows, cols)
    big = tuple(
        pltpu.with_memory_space_constraint(x, pltpu.HBM) for x in (features, state, cs, wu, wr, wc, u_state)
    )
    small = tuple(
        pltpu.with_memory_space_constraint(x, pltpu.HBM) for x in (live, nbrs.T, perm, bu, br, bc, b_coarse)
    )
    fine = jax.ShapeDtypeStruct((bands, slots, half, rows, cols), F32)
    pooled = jax.ShapeDtypeStruct((nb * nr, cr * half, cols), F32)
    coarse = jax.ShapeDtypeStruct((2, chans, cr * cols), F32)
    new, parts, held = pl.pallas_call(
        functools.partial(kernel, nt, nb, nr, ins, rows),
        out_shape=(fine, pooled, coarse),
        in_specs=[hbm] * (len(small) + len(big)),
        out_specs=(vm, vm, vm),
        scratch_shapes=[pltpu.SMEM(x.shape, x.dtype) for x in small]
        + [pltpu.VMEM(x.shape, x.dtype) for x in big]
        + [
            pltpu.VMEM((bands, slots, ins * rows, cols), F32),
            pltpu.VMEM((bands, 3, slab, cols), BF16),
            pltpu.VMEM((bands, 3, slab, cols), BF16),
            pltpu.VMEM((bands, 3, slab, cols), BF16),
            pltpu.VMEM((bands, 3, slab, cols), BF16),
            pltpu.VMEM((slots + 2, bands, slab, cols), BF16),
            pltpu.VMEM((slots + 2, bands, slab, cols), BF16),
            pltpu.VMEM((slots + 2, bands, 2, slab, cols), BF16),
            pltpu.VMEM((slots + 2, bands, 2, slab, cols), BF16),
            pltpu.VMEM((k3, 2 * bands * cols), BF16),
            pltpu.VMEM((slots, bands, (half + chans) * rows, cols), F32),
            pltpu.VMEM((6, chans, k1), F32),
            pltpu.VMEM((3, chans, k2), F32),
            pltpu.VMEM((3, chans, k3), F32),
            pltpu.VMEM(((half + chans) * rows, k1), BF16),
            pltpu.VMEM((half * rows, k2), BF16),
            pltpu.VMEM((2 * chans, k3), BF16),
            pltpu.VMEM((slots, k1, bands * cols), BF16),
            pltpu.VMEM((slots, k2, bands * cols), BF16),
            pltpu.SemaphoreType.DMA((len(small) + len(big),)),
            pltpu.SemaphoreType.DMA((2,)),
            pltpu.SemaphoreType.DMA((2,)),
            pltpu.SemaphoreType.DMA((nb * nr - 1,)),
            pltpu.SemaphoreType.DMA((nb * nr - 1,)),
        ],
        compiler_params=pltpu.CompilerParams(
            collective_id=0, has_side_effects=True, vmem_limit_bytes=24 * 1024 * 1024
        ),
    )(*small, *big)
    return pl.pallas_call(
        functools.partial(finish, nb, nr, cs.shape[0]),
        out_shape=(fine, jax.ShapeDtypeStruct(cs.shape, F32)),
        in_specs=[vm, vm, vm, pl.BlockSpec(memory_space=pl.ANY)],
        out_specs=(hbm, hbm),
        scratch_shapes=[
            pltpu.VMEM(cs.shape, F32),
            pltpu.SemaphoreType.DMA((bands * slots + 1,)),
        ],
        compiler_params=pltpu.CompilerParams(vmem_limit_bytes=24 * 1024 * 1024),
    )(parts, held, u_pool, new)


def solution(mesh):
    nt, nb, nr = mesh.shape["tiles"], mesh.shape["band"], mesh.shape["rep"]
    return jax.shard_map(
        functools.partial(shards, nt, nb, nr),
        mesh=mesh,
        in_specs=(
            P(("groups", "band"), "tiles", None, None, None),
            P(("groups", "band"), "tiles", None, None, None),
            P("tiles"),
            P("tiles", None),
            P("tiles", None),
            P(("groups", "tiles", "band"), None, None, None),
            P(),
            P(),
            P(),
            P(),
            P(),
            P(),
            P(),
            P(),
            P(),
        ),
        out_specs=(
            P(("groups", "band"), "tiles", "rep", None, None),
            P(("groups", "tiles", "band"), None, None, None),
        ),
        check_vma=False,
    )
```

```python
import functools

import jax
import jax.numpy as jnp
from jax import lax
from jax.experimental import pallas as pl
from jax.experimental.pallas import tpu as pltpu
from jax.sharding import PartitionSpec as P

MESH = pl.DeviceIdType.MESH
HIGHEST = lax.Precision.HIGHEST
F32 = jnp.float32
BF16 = jnp.bfloat16


def iota(shape, dim):
    return lax.broadcasted_iota(jnp.int32, shape, dim)


def sigmoid(x):
    return 0.5 * jnp.tanh(0.5 * x) + 0.5


def thirds(x):
    high = x.astype(BF16)
    rest = x - high.astype(F32)
    middle = rest.astype(BF16)
    return high, middle, (rest - middle.astype(F32)).astype(BF16)


def shifted(x, step):
    width = x.shape[1]
    wide = pltpu.roll(x, (-step) % width, 1).reshape(-1, 16, width)
    column = iota((16, width), 1) + step
    keep = ((column >= 0) & (column < width)).astype(F32).astype(BF16)
    return (wide * keep[None]).reshape(x.shape)


def kernel(
    nt, nb, nr, ins, rows,
    live_in, nbrs_in, perm_in, bu_in, br_in, bc_in, b_coarse_in, features_in, state_in, cs_in, wu_in, wr_in, wc_in, u_state_in,
    out, parts, coarse,
    live, nbrs, perm, bu, br, bc, b_coarse, features, state, cs, wu, wr, wc, u_state,
    feats, send_up, send_dn, got_up, got_dn, tops, bots, gtops, gbots, strip, gates,
    w1, w2, w3, t1, t2, t3, x1, x2,
    load_sems, up_sems, dn_sems, pool_send, pool_recv,
):
    bands, slots, flat, cols = state.shape
    chans = flat // rows
    half = chans // nr
    width = ins + chans
    own, cr, cw = cs.shape[0], cs.shape[2], cs.shape[3]
    km = width * rows
    slab = strip.shape[0] // 12
    tile = lax.axis_index("tiles")
    band = lax.axis_index("band")
    rep = lax.axis_index("rep")
    base = tile * slots
    npeer = nb * nr
    me = band * nr + rep
    start = rep * half

    loads = [
        pltpu.make_async_copy(src, dst, load_sems.at[i])
        for i, (src, dst) in enumerate(
            (
                (wu_in, wu), (wr_in, wr), (wc_in, wc), (features_in, features),
                (cs_in, cs), (u_state_in, u_state),
                (live_in, live), (nbrs_in, nbrs), (perm_in, perm),
                (bu_in, bu), (br_in, br), (bc_in, bc), (b_coarse_in, b_coarse),
            )
        )
    ]
    state_loads = [
        pltpu.make_async_copy(state_in.at[b, s], state.at[b, s], load_sems.at[len(loads) + b * slots + s])
        for b in range(bands)
        for s in range(slots)
    ]
    for load in loads[:4] + state_loads + loads[4:]:
        load.start()

    barrier = pltpu.get_barrier_semaphore()
    has_up, has_dn = tile > 0, tile < nt - 1

    @pl.when(has_up)
    def _():
        pl.semaphore_signal(barrier, inc=1, device_id={"tiles": tile - 1}, device_id_type=MESH)

    @pl.when(has_dn)
    def _():
        pl.semaphore_signal(barrier, inc=1, device_id={"tiles": tile + 1}, device_id_type=MESH)

    for d in range(1, npeer):
        peer = lax.rem(me + d, npeer)
        pl.semaphore_signal(
            barrier, inc=1, device_id={"band": peer // nr, "rep": lax.rem(peer, nr)}, device_id_type=MESH
        )

    def lanes(size, main, halo):
        part = size // 3
        k = iota((1, size), 1)
        side = (k >= part).astype(jnp.int32) + (k >= 2 * part).astype(jnp.int32)
        q = k - part * side
        h = q - main
        chan = jnp.where(h >= 0, h & (slab - 1), q >> 4)
        row = q & (rows - 1)
        for j, at in enumerate(halo):
            row = jnp.where(h >= j * slab, at, row)
        entry = jnp.where(chan < chans, chan + ins, chan - chans)
        return jnp.where(chan < width, entry + 32 * side, -1), row

    def spread(target, weights, main, halo):
        size = target.shape[2]
        entry, _ = lanes(size, main, halo)
        total = jnp.zeros((3 * chans * len(weights), size), F32)
        for b in range(3):
            stack = jnp.concatenate([w[3 * a + b] for w in weights for a in range(3)], axis=0)
            pick = (entry == iota((width, size), 0) + 32 * b).astype(F32).astype(BF16)
            total = total + jnp.dot(stack, pick, preferred_element_type=F32)
        target[...] = total.reshape(target.shape)

    def fill(target, source, jobs, main, halo, dilation):
        shape = (rows, target.shape[1])
        _, row = lanes(shape[1], main, halo)
        delta = row - iota(shape, 0)
        hits = [(delta == a * dilation).astype(F32).astype(BF16) for a in (-1, 0, 1)]
        for at, gate, outs, count in jobs:
            for o in range(count):
                total = None
                for a in range(3):
                    line = jnp.broadcast_to(source[3 * gate + a, pl.ds(outs + o, 1), :], shape).astype(BF16)
                    total = line * hits[a] if total is None else total + line * hits[a]
                target[at + o * rows : at + (o + 1) * rows, :] = total

    mu = half * rows
    halo1, halo2, halo3 = (-1, rows), (-2, -1, rows, rows + 1), (-3, -2, -1, 0)
    for load in loads[:3]:
        load.wait()
    spread(w1, (wu, wr), km, halo1)
    spread(w2, (wc,), km, halo2)
    spread(w3, (wr,), 0, halo3)
    for load in loads[6:]:
        load.wait()
    first = jnp.int32(0)
    last = jnp.int32(0)
    for s in range(slots):
        u, d = nbrs[0, s], nbrs[1, s]
        alive = live[s] > 0
        first = jnp.where(alive & ((u < base) | (u >= base + slots)), s, first)
        last = jnp.where(alive & ((d < base) | (d >= base + slots)), s, last)

    for load in loads[3:4] + state_loads:
        load.wait()
    for s in range(slots):
        for b in range(bands):
            feats[b, s] = features[b, s].astype(F32)

    blank = jnp.zeros((slab - width, cols), F32)

    def feat_rows(b, s, row):
        return jnp.concatenate([feats[b, s, ch * rows + row : ch * rows + row + 1] for ch in range(ins)] + [blank], axis=0)

    def row_slab(b, s, row):
        return jnp.concatenate([state[b, s, pl.ds(row, chans, stride=rows), :], feat_rows(b, s, row)], axis=0).astype(BF16)

    for b in range(bands):
        for i in range(3):
            send_up[b, i] = row_slab(b, first, i)
            send_dn[b, i] = row_slab(b, last, rows - 3 + i)

    pl.semaphore_wait(barrier, npeer - 1 + jnp.where(has_up, 1, 0) + jnp.where(has_dn, 1, 0))

    def copy_up():
        return pltpu.make_async_remote_copy(
            send_up, got_dn, up_sems.at[0], up_sems.at[1], device_id={"tiles": tile - 1}, device_id_type=MESH
        )

    def copy_dn():
        return pltpu.make_async_remote_copy(
            send_dn, got_up, dn_sems.at[0], dn_sems.at[1], device_id={"tiles": tile + 1}, device_id_type=MESH
        )

    @pl.when(has_up)
    def _():
        copy_up().start()

    @pl.when(has_dn)
    def _():
        copy_dn().start()

    @pl.when(jnp.logical_not(has_up))
    def _():
        got_up[...] = jnp.zeros_like(got_up)

    @pl.when(jnp.logical_not(has_dn))
    def _():
        got_dn[...] = jnp.zeros_like(got_dn)

    fill(t1, w1, ((0, 0, start, half), (mu, 1, 0, chans)), km, halo1, 1)
    fill(t2, w2, ((0, 0, start, half),), km, halo2, 2)
    _, row3 = lanes(t3.shape[1], 0, halo3)
    for i in range(2):
        total = jnp.zeros((chans, t3.shape[1]), F32)
        for a in range(3):
            total = jnp.where(row3 == i - 2 + a - 1, w3[a], total)
        t3[i * chans : (i + 1) * chans] = total.astype(BF16)

    for load in loads[4:6]:
        load.wait()
    coarse[0] = jnp.zeros_like(coarse[0])
    for k in range(own):
        for i in range(cr):
            coarse[0, :, i * cols + k * cw : i * cols + (k + 1) * cw] = cs[k, :, i, :]
    coarse_bias = jnp.zeros((chans, 1), F32)
    for o in range(chans):
        coarse_bias = jnp.where(iota((chans, 1), 0) == o, b_coarse[o], coarse_bias)
    coarse[1] = jnp.dot(u_state[...], coarse[0], precision=HIGHEST, preferred_element_type=F32) + coarse_bias

    k1, k2 = km + 2 * slab, km + 4 * slab
    for s in range(slots):
        for b in range(bands):
            at = slice(b * cols, (b + 1) * cols)
            tops[s, b] = row_slab(b, s, 0)
            bots[s, b] = row_slab(b, s, rows - 1)
            x = state[b, s].astype(BF16)
            f = features[b, s]
            for j, step in enumerate((-1, 0, 1)):
                x1[s, j * k1 : j * k1 + flat, at] = shifted(x, step) if step else x
                x1[s, j * k1 + flat : j * k1 + km, at] = shifted(f, step) if step else f
                x2[s, j * k2 + flat : j * k2 + km, at] = shifted(f, 2 * step) if step else f
    tops[slots + 1] = jnp.zeros((bands, slab, cols), BF16)
    bots[slots + 1] = jnp.zeros((bands, slab, cols), BF16)
    gtops[slots + 1] = jnp.zeros((bands, 2, slab, cols), BF16)
    gbots[slots + 1] = jnp.zeros((bands, 2, slab, cols), BF16)
    edge_up = [row_slab(b, first, 0) for b in range(bands)]
    edge_dn = [row_slab(b, last, rows - 1) for b in range(bands)]

    @pl.when(has_up)
    def _():
        copy_up().wait_send()

    @pl.when(has_dn)
    def _():
        copy_up().wait_recv()

    @pl.when(has_dn)
    def _():
        copy_dn().wait_send()

    @pl.when(has_up)
    def _():
        copy_dn().wait_recv()

    for b in range(bands):
        bots[slots, b] = got_up[b, 2]
        tops[slots, b] = got_dn[b, 0]

    def place(s, side):
        n = nbrs[side, s]
        here = (n >= base) & (n < base + slots)
        return jnp.where(here, n - base, jnp.where(n >= 0, slots, slots + 1))

    updates = []
    for s in range(slots):
        above, below = place(s, 0), place(s, 1)
        for b in range(bands):
            at = slice(b * cols, (b + 1) * cols)
            x = jnp.concatenate([bots[above, b], tops[below, b]], axis=0)
            for j, step in enumerate((-1, 0, 1)):
                x1[s, j * k1 + km : (j + 1) * k1, at] = shifted(x, step) if step else x
        acc = jnp.dot(t1[...], x1[s], preferred_element_type=F32)
        for b in range(bands):
            at = slice(b * cols, (b + 1) * cols)
            for o in range(half):
                gates[s, b, o * rows : (o + 1) * rows] = sigmoid(acc[o * rows : (o + 1) * rows, at] + bu[start + o])
            for o in range(chans):
                reset = sigmoid(acc[mu + o * rows : mu + (o + 1) * rows, at] + br[o])
                held = state[b, s, o * rows : (o + 1) * rows].astype(BF16).astype(F32)
                gates[s, b, mu + o * rows : mu + (o + 1) * rows] = reset * held
            x = gates[s, b, mu:].astype(BF16)
            for j, step in enumerate((-1, 0, 1)):
                x2[s, j * k2 : j * k2 + flat, at] = shifted(x, 2 * step) if step else x
            for i in range(2):
                for target, row in ((gtops, i), (gbots, rows - 2 + i)):
                    g = gates[s, b, pl.ds(mu + row, chans, stride=rows), :]
                    target[s, b, i] = jnp.concatenate([g, feat_rows(b, s, row)], axis=0).astype(BF16)

    for b in range(bands):
        for side in range(2):
            four = [got_up[b, i] for i in range(3)] + [edge_up[b]] if side == 0 else [edge_dn[b]] + [got_dn[b, i] for i in range(3)]
            at = slice((2 * side + b) * cols, (2 * side + b + 1) * cols)
            x = jnp.concatenate(four, axis=0)
            strip[0 : 4 * slab, at] = shifted(x, -1)
            strip[4 * slab : 8 * slab, at] = x
            strip[8 * slab :, at] = shifted(x, 1)
    acc = jnp.dot(t3[...], strip[...], preferred_element_type=F32)
    reset_bias = jnp.zeros((chans, 1), F32)
    for o in range(chans):
        reset_bias = jnp.where(iota((chans, 1), 0) == o, br[o], reset_bias)
    for b in range(bands):
        for side in range(2):
            at = slice((2 * side + b) * cols, (2 * side + b + 1) * cols)
            for i in range(2):
                held = (got_up[b, 1 + i] if side == 0 else got_dn[b, i]).astype(F32)
                reset = sigmoid(acc[i * chans : (i + 1) * chans, at] + reset_bias)
                joined = jnp.concatenate([reset * held[:chans], held[chans:]], axis=0).astype(BF16)
                if side == 0:
                    gbots[slots, b, i] = joined
                else:
                    gtops[slots, b, i] = joined

    pooled = jnp.zeros((mu, slots * cw), F32)
    for s in range(slots):
        above, below = place(s, 0), place(s, 1)
        for b in range(bands):
            at = slice(b * cols, (b + 1) * cols)
            x = jnp.concatenate([gbots[above, b, 0], gbots[above, b, 1], gtops[below, b, 0], gtops[below, b, 1]], axis=0)
            for j, step in enumerate((-1, 0, 1)):
                x2[s, j * k2 + km : (j + 1) * k2, at] = shifted(x, 2 * step) if step else x
        acc = jnp.dot(t2[...], x2[s], preferred_element_type=F32)
        scale = live[s].astype(F32)
        summed = []
        for o in range(half):
            both = None
            for b in range(bands):
                at = slice(b * cols, (b + 1) * cols)
                update = gates[s, b, o * rows : (o + 1) * rows]
                cand = jnp.tanh(acc[o * rows : (o + 1) * rows, at] + bc[start + o])
                held = state[b, s, pl.ds(pl.multiple_of((start + o) * rows, rows), rows), :]
                new = ((1.0 - update) * held + update * cand) * scale
                out[b, s, o] = new
                both = new if both is None else both + new
            summed.append(both)
        summed = jnp.concatenate(summed, axis=0)
        spot = jnp.int32(0)
        for k in range(slots):
            spot = jnp.where(perm[0, k] == s, k, spot)
        gather = jnp.where(
            iota((cols, slots * cw), 1) == spot * cw + (iota((cols, slots * cw), 0) >> 2), 1.0 / 16.0, 0.0
        )
        product = jnp.dot(jnp.concatenate(thirds(summed), axis=0), gather.astype(BF16), preferred_element_type=F32)
        pooled = pooled + (product[:mu] + (product[mu : 2 * mu] + product[2 * mu :]))

    m, q = iota((cr * half, mu), 0), iota((cr * half, mu), 1)
    rowsum = jnp.where(((m & (half - 1)) == (q >> 4)) & ((m >> (half.bit_length() - 1)) == ((q & (rows - 1)) >> 2)), 1.0, 0.0)
    product = jnp.dot(rowsum.astype(BF16), jnp.concatenate(thirds(pooled), axis=1), preferred_element_type=F32)
    parts[me] = product[:, :cols] + (product[:, cols : 2 * cols] + product[:, 2 * cols :])

    copies = []
    for d in range(1, npeer):
        peer = lax.rem(me + d, npeer)
        copy = pltpu.make_async_remote_copy(
            parts.at[me], parts.at[me], pool_send.at[d - 1], pool_recv.at[d - 1],
            device_id={"band": peer // nr, "rep": lax.rem(peer, nr)}, device_id_type=MESH,
        )
        copy.start()
        copies.append(copy)
    for copy in copies:
        copy.wait()


def finish(
    nb, nr, own, parts, coarse, u_pool, new_in, out, coarse_out, cout, store_sems
):
    bands, slots, half = new_in.shape[:3]
    cr, cw = cout.shape[2], cout.shape[3]
    cols = slots * cw
    band = lax.axis_index("band")
    stores = []
    for b in range(bands):
        for s in range(slots):
            stores.append(pltpu.make_async_copy(new_in.at[b, s], out.at[b, s], store_sems.at[b * slots + s]))
            stores[-1].start()
    halves = []
    for r in range(nr):
        total = parts[r]
        for b in range(1, nb):
            total = total + parts[b * nr + r]
        halves.append(pltpu.roll(total, lax.rem(cols - band * (own * cw), cols), 1))
    wide = jnp.concatenate(
        [jnp.concatenate([x[i * half : (i + 1) * half] for x in halves], axis=0) for i in range(cr)], axis=1
    )
    pre = coarse[1] + jnp.dot(u_pool[...], wide, precision=HIGHEST, preferred_element_type=F32)
    new = coarse[0] + jnp.tanh(pre)
    for k in range(own):
        for i in range(cr):
            cout[k, :, i, :] = new[:, i * cols + k * cw : i * cols + (k + 1) * cw]
    stores.append(pltpu.make_async_copy(cout, coarse_out, store_sems.at[bands * slots]))
    stores[-1].start()
    for store in stores:
        store.wait()


def shards(nt, nb, nr, features, state, live, nbrs, perm, cs, wu, bu, wr, br, wc, bc, u_pool, u_state, b_coarse):
    bands, slots, chans, rows, cols = state.shape
    ins = features.shape[2]
    width = ins + chans
    half = chans // nr
    km = width * rows
    slab = 32
    k1, k2, k3 = 3 * (km + 2 * slab), 3 * (km + 4 * slab), 12 * slab
    cr = rows // 4
    hbm = pl.BlockSpec(memory_space=pltpu.HBM)
    vm = pl.BlockSpec(memory_space=pltpu.VMEM)
    features = features.reshape(bands, slots, ins * rows, cols)
    state = state.reshape(bands, slots, chans * rows, cols)
    big = tuple(
        pltpu.with_memory_space_constraint(x, pltpu.HBM) for x in (features, state, cs, wu, wr, wc, u_state)
    )
    small = tuple(
        pltpu.with_memory_space_constraint(x, pltpu.HBM) for x in (live, nbrs.T, perm, bu, br, bc, b_coarse)
    )
    fine = jax.ShapeDtypeStruct((bands, slots, half, rows, cols), F32)
    pooled = jax.ShapeDtypeStruct((nb * nr, cr * half, cols), F32)
    coarse = jax.ShapeDtypeStruct((2, chans, cr * cols), F32)
    new, parts, held = pl.pallas_call(
        functools.partial(kernel, nt, nb, nr, ins, rows),
        out_shape=(fine, pooled, coarse),
        in_specs=[hbm] * (len(small) + len(big)),
        out_specs=(vm, vm, vm),
        scratch_shapes=[pltpu.SMEM(x.shape, x.dtype) for x in small]
        + [pltpu.VMEM(x.shape, x.dtype) for x in big]
        + [
            pltpu.VMEM((bands, slots, ins * rows, cols), F32),
            pltpu.VMEM((bands, 3, slab, cols), BF16),
            pltpu.VMEM((bands, 3, slab, cols), BF16),
            pltpu.VMEM((bands, 3, slab, cols), BF16),
            pltpu.VMEM((bands, 3, slab, cols), BF16),
            pltpu.VMEM((slots + 2, bands, slab, cols), BF16),
            pltpu.VMEM((slots + 2, bands, slab, cols), BF16),
            pltpu.VMEM((slots + 2, bands, 2, slab, cols), BF16),
            pltpu.VMEM((slots + 2, bands, 2, slab, cols), BF16),
            pltpu.VMEM((k3, 2 * bands * cols), BF16),
            pltpu.VMEM((slots, bands, (half + chans) * rows, cols), F32),
            pltpu.VMEM((6, chans, k1), F32),
            pltpu.VMEM((3, chans, k2), F32),
            pltpu.VMEM((3, chans, k3), F32),
            pltpu.VMEM(((half + chans) * rows, k1), BF16),
            pltpu.VMEM((half * rows, k2), BF16),
            pltpu.VMEM((2 * chans, k3), BF16),
            pltpu.VMEM((slots, k1, bands * cols), BF16),
            pltpu.VMEM((slots, k2, bands * cols), BF16),
            pltpu.SemaphoreType.DMA((len(small) + len(big) + bands * slots,)),
            pltpu.SemaphoreType.DMA((2,)),
            pltpu.SemaphoreType.DMA((2,)),
            pltpu.SemaphoreType.DMA((nb * nr - 1,)),
            pltpu.SemaphoreType.DMA((nb * nr - 1,)),
        ],
        compiler_params=pltpu.CompilerParams(
            collective_id=0, has_side_effects=True, vmem_limit_bytes=24 * 1024 * 1024
        ),
    )(*small, *big)
    return pl.pallas_call(
        functools.partial(finish, nb, nr, cs.shape[0]),
        out_shape=(fine, jax.ShapeDtypeStruct(cs.shape, F32)),
        in_specs=[vm, vm, vm, pl.BlockSpec(memory_space=pl.ANY)],
        out_specs=(hbm, hbm),
        scratch_shapes=[
            pltpu.VMEM(cs.shape, F32),
            pltpu.SemaphoreType.DMA((bands * slots + 1,)),
        ],
        compiler_params=pltpu.CompilerParams(vmem_limit_bytes=24 * 1024 * 1024),
    )(parts, held, u_pool, new)


def solution(mesh):
    nt, nb, nr = mesh.shape["tiles"], mesh.shape["band"], mesh.shape["rep"]
    return jax.shard_map(
        functools.partial(shards, nt, nb, nr),
        mesh=mesh,
        in_specs=(
            P(("groups", "band"), "tiles", None, None, None),
            P(("groups", "band"), "tiles", None, None, None),
            P("tiles"),
            P("tiles", None),
            P("tiles", None),
            P(("groups", "tiles", "band"), None, None, None),
            P(),
            P(),
            P(),
            P(),
            P(),
            P(),
            P(),
            P(),
            P(),
        ),
        out_specs=(
            P(("groups", "band"), "tiles", "rep", None, None),
            P(("groups", "tiles", "band"), None, None, None),
        ),
        check_vma=False,
    )
```

```python
import functools

import jax
import jax.numpy as jnp
from jax import lax
from jax.experimental import pallas as pl
from jax.experimental.pallas import tpu as pltpu
from jax.sharding import PartitionSpec as P

MESH = pl.DeviceIdType.MESH
HIGHEST = lax.Precision.HIGHEST
F32 = jnp.float32
BF16 = jnp.bfloat16


def iota(shape, dim):
    return lax.broadcasted_iota(jnp.int32, shape, dim)


def sigmoid(x):
    return 0.5 * jnp.tanh(0.5 * x) + 0.5


def thirds(x):
    high = x.astype(BF16)
    rest = x - high.astype(F32)
    middle = rest.astype(BF16)
    return high, middle, (rest - middle.astype(F32)).astype(BF16)


def shifted(x, step):
    width = x.shape[1]
    wide = pltpu.roll(x, (-step) % width, 1).reshape(-1, 16, width)
    column = iota((16, width), 1) + step
    keep = ((column >= 0) & (column < width)).astype(F32).astype(BF16)
    return (wide * keep[None]).reshape(x.shape)


def kernel(
    nt, nb, nr, ins, rows,
    live_in, nbrs_in, perm_in, bu_in, br_in, bc_in, b_coarse_in, features_in, state_in, cs_in, wu_in, wr_in, wc_in, u_state_in,
    out, parts, coarse,
    live, nbrs, perm, bu, br, bc, b_coarse, features, state, cs, wu, wr, wc, u_state,
    feats, send_up, send_dn, got_up, got_dn, tops, bots, gtops, gbots, strip, gates,
    w1, w2, w3, t1, t2, t3, x1, x2,
    load_sems, up_sems, dn_sems, pool_send, pool_recv,
):
    bands, slots, flat, cols = state.shape
    chans = flat // rows
    half = chans // nr
    width = ins + chans
    own, cr, cw = cs.shape[0], cs.shape[2], cs.shape[3]
    km = width * rows
    slab = strip.shape[0] // 12
    tile = lax.axis_index("tiles")
    band = lax.axis_index("band")
    rep = lax.axis_index("rep")
    base = tile * slots
    npeer = nb * nr
    me = band * nr + rep
    start = rep * half

    loads = [
        pltpu.make_async_copy(src, dst, load_sems.at[i])
        for i, (src, dst) in enumerate(
            (
                (wu_in, wu), (wr_in, wr), (wc_in, wc), (features_in, features),
                (cs_in, cs), (u_state_in, u_state),
                (live_in, live), (nbrs_in, nbrs), (perm_in, perm),
                (bu_in, bu), (br_in, br), (bc_in, bc), (b_coarse_in, b_coarse),
            )
        )
    ]
    state_loads = [
        pltpu.make_async_copy(state_in.at[b, s], state.at[b, s], load_sems.at[len(loads) + b * slots + s])
        for b in range(bands)
        for s in range(slots)
    ]
    for load in loads[:4] + state_loads + loads[4:]:
        load.start()

    barrier = pltpu.get_barrier_semaphore()
    has_up, has_dn = tile > 0, tile < nt - 1

    @pl.when(has_up)
    def _():
        pl.semaphore_signal(barrier, inc=1, device_id={"tiles": tile - 1}, device_id_type=MESH)

    @pl.when(has_dn)
    def _():
        pl.semaphore_signal(barrier, inc=1, device_id={"tiles": tile + 1}, device_id_type=MESH)

    for d in range(1, npeer):
        peer = lax.rem(me + d, npeer)
        pl.semaphore_signal(
            barrier, inc=1, device_id={"band": peer // nr, "rep": lax.rem(peer, nr)}, device_id_type=MESH
        )

    def lanes(size, main, halo):
        part = size // 3
        k = iota((1, size), 1)
        side = (k >= part).astype(jnp.int32) + (k >= 2 * part).astype(jnp.int32)
        q = k - part * side
        h = q - main
        chan = jnp.where(h >= 0, h & (slab - 1), q >> 4)
        row = q & (rows - 1)
        for j, at in enumerate(halo):
            row = jnp.where(h >= j * slab, at, row)
        entry = jnp.where(chan < chans, chan + ins, chan - chans)
        return jnp.where(chan < width, entry + 32 * side, -1), row

    def spread(target, weights, main, halo):
        size = target.shape[2]
        entry, _ = lanes(size, main, halo)
        total = jnp.zeros((3 * chans * len(weights), size), F32)
        for b in range(3):
            stack = jnp.concatenate([w[3 * a + b] for w in weights for a in range(3)], axis=0)
            pick = (entry == iota((width, size), 0) + 32 * b).astype(F32).astype(BF16)
            total = total + jnp.dot(stack, pick, preferred_element_type=F32)
        target[...] = total.reshape(target.shape)

    def fill(target, source, jobs, main, halo, dilation):
        shape = (rows, target.shape[1])
        _, row = lanes(shape[1], main, halo)
        delta = row - iota(shape, 0)
        hits = [(delta == a * dilation).astype(F32).astype(BF16) for a in (-1, 0, 1)]
        for at, gate, outs, count in jobs:

            def step(o, carry, at=at, gate=gate, outs=outs):
                total = None
                for a in range(3):
                    line = jnp.broadcast_to(source[3 * gate + a, pl.ds(outs + o, 1), :], shape).astype(BF16)
                    total = line * hits[a] if total is None else total + line * hits[a]
                target[pl.ds(pl.multiple_of(at + o * rows, rows), rows), :] = total
                return carry

            lax.fori_loop(0, count, step, 0, unroll=2)

    mu = half * rows
    halo1, halo2, halo3 = (-1, rows), (-2, -1, rows, rows + 1), (-3, -2, -1, 0)
    for load in loads[:3]:
        load.wait()
    spread(w1, (wu, wr), km, halo1)
    spread(w2, (wc,), km, halo2)
    spread(w3, (wr,), 0, halo3)
    for load in loads[6:]:
        load.wait()
    first = jnp.int32(0)
    last = jnp.int32(0)
    for s in range(slots):
        u, d = nbrs[0, s], nbrs[1, s]
        alive = live[s] > 0
        first = jnp.where(alive & ((u < base) | (u >= base + slots)), s, first)
        last = jnp.where(alive & ((d < base) | (d >= base + slots)), s, last)

    for load in loads[3:4] + state_loads:
        load.wait()
    for s in range(slots):
        for b in range(bands):
            feats[b, s] = features[b, s].astype(F32)

    blank = jnp.zeros((slab - width, cols), F32)

    def feat_rows(b, s, row):
        return jnp.concatenate([feats[b, s, ch * rows + row : ch * rows + row + 1] for ch in range(ins)] + [blank], axis=0)

    def row_slab(b, s, row):
        return jnp.concatenate([state[b, s, pl.ds(row, chans, stride=rows), :], feat_rows(b, s, row)], axis=0).astype(BF16)

    for b in range(bands):
        for i in range(3):
            send_up[b, i] = row_slab(b, first, i)
            send_dn[b, i] = row_slab(b, last, rows - 3 + i)

    pl.semaphore_wait(barrier, npeer - 1 + jnp.where(has_up, 1, 0) + jnp.where(has_dn, 1, 0))

    def copy_up():
        return pltpu.make_async_remote_copy(
            send_up, got_dn, up_sems.at[0], up_sems.at[1], device_id={"tiles": tile - 1}, device_id_type=MESH
        )

    def copy_dn():
        return pltpu.make_async_remote_copy(
            send_dn, got_up, dn_sems.at[0], dn_sems.at[1], device_id={"tiles": tile + 1}, device_id_type=MESH
        )

    @pl.when(has_up)
    def _():
        copy_up().start()

    @pl.when(has_dn)
    def _():
        copy_dn().start()

    @pl.when(jnp.logical_not(has_up))
    def _():
        got_up[...] = jnp.zeros_like(got_up)

    @pl.when(jnp.logical_not(has_dn))
    def _():
        got_dn[...] = jnp.zeros_like(got_dn)

    fill(t1, w1, ((0, 0, start, half), (mu, 1, 0, chans)), km, halo1, 1)
    fill(t2, w2, ((0, 0, start, half),), km, halo2, 2)
    _, row3 = lanes(t3.shape[1], 0, halo3)
    for i in range(2):
        total = jnp.zeros((chans, t3.shape[1]), F32)
        for a in range(3):
            total = jnp.where(row3 == i - 2 + a - 1, w3[a], total)
        t3[i * chans : (i + 1) * chans] = total.astype(BF16)

    for load in loads[4:6]:
        load.wait()
    coarse[0] = jnp.zeros_like(coarse[0])
    for k in range(own):
        for i in range(cr):
            coarse[0, :, i * cols + k * cw : i * cols + (k + 1) * cw] = cs[k, :, i, :]
    coarse_bias = jnp.zeros((chans, 1), F32)
    for o in range(chans):
        coarse_bias = jnp.where(iota((chans, 1), 0) == o, b_coarse[o], coarse_bias)
    coarse[1] = jnp.dot(u_state[...], coarse[0], precision=HIGHEST, preferred_element_type=F32) + coarse_bias

    k1, k2 = km + 2 * slab, km + 4 * slab
    def prepare(s, carry):
        for b in range(bands):
            at = slice(b * cols, (b + 1) * cols)
            tops[s, b] = row_slab(b, s, 0)
            bots[s, b] = row_slab(b, s, rows - 1)
            x = state[b, s].astype(BF16)
            f = features[b, s]
            for j, step in enumerate((-1, 0, 1)):
                x1[s, j * k1 : j * k1 + flat, at] = shifted(x, step) if step else x
                x1[s, j * k1 + flat : j * k1 + km, at] = shifted(f, step) if step else f
                x2[s, j * k2 + flat : j * k2 + km, at] = shifted(f, 2 * step) if step else f
        return carry

    lax.fori_loop(0, slots, prepare, 0)

    tops[slots + 1] = jnp.zeros((bands, slab, cols), BF16)
    bots[slots + 1] = jnp.zeros((bands, slab, cols), BF16)
    gtops[slots + 1] = jnp.zeros((bands, 2, slab, cols), BF16)
    gbots[slots + 1] = jnp.zeros((bands, 2, slab, cols), BF16)
    edge_up = [row_slab(b, first, 0) for b in range(bands)]
    edge_dn = [row_slab(b, last, rows - 1) for b in range(bands)]

    @pl.when(has_up)
    def _():
        copy_up().wait_send()

    @pl.when(has_dn)
    def _():
        copy_up().wait_recv()

    @pl.when(has_dn)
    def _():
        copy_dn().wait_send()

    @pl.when(has_up)
    def _():
        copy_dn().wait_recv()

    for b in range(bands):
        bots[slots, b] = got_up[b, 2]
        tops[slots, b] = got_dn[b, 0]

    def place(s, side):
        n = nbrs[side, s]
        here = (n >= base) & (n < base + slots)
        return jnp.where(here, n - base, jnp.where(n >= 0, slots, slots + 1))

    def gate(s, carry):
        above, below = place(s, 0), place(s, 1)
        for b in range(bands):
            at = slice(b * cols, (b + 1) * cols)
            x = jnp.concatenate([bots[above, b], tops[below, b]], axis=0)
            for j, step in enumerate((-1, 0, 1)):
                x1[s, j * k1 + km : (j + 1) * k1, at] = shifted(x, step) if step else x
        acc = jnp.dot(t1[...], x1[s], preferred_element_type=F32)
        for b in range(bands):
            at = slice(b * cols, (b + 1) * cols)
            for o in range(half):
                gates[s, b, o * rows : (o + 1) * rows] = sigmoid(acc[o * rows : (o + 1) * rows, at] + bu[start + o])
            for o in range(chans):
                reset = sigmoid(acc[mu + o * rows : mu + (o + 1) * rows, at] + br[o])
                held = state[b, s, o * rows : (o + 1) * rows].astype(BF16).astype(F32)
                gates[s, b, mu + o * rows : mu + (o + 1) * rows] = reset * held
            x = gates[s, b, mu:].astype(BF16)
            for j, step in enumerate((-1, 0, 1)):
                x2[s, j * k2 : j * k2 + flat, at] = shifted(x, 2 * step) if step else x
            for i in range(2):
                for target, row in ((gtops, i), (gbots, rows - 2 + i)):
                    g = gates[s, b, pl.ds(mu + row, chans, stride=rows), :]
                    target[s, b, i] = jnp.concatenate([g, feat_rows(b, s, row)], axis=0).astype(BF16)
        return carry

    lax.fori_loop(0, slots, gate, 0)

    for b in range(bands):
        for side in range(2):
            four = [got_up[b, i] for i in range(3)] + [edge_up[b]] if side == 0 else [edge_dn[b]] + [got_dn[b, i] for i in range(3)]
            at = slice((2 * side + b) * cols, (2 * side + b + 1) * cols)
            x = jnp.concatenate(four, axis=0)
            strip[0 : 4 * slab, at] = shifted(x, -1)
            strip[4 * slab : 8 * slab, at] = x
            strip[8 * slab :, at] = shifted(x, 1)
    acc = jnp.dot(t3[...], strip[...], preferred_element_type=F32)
    reset_bias = jnp.zeros((chans, 1), F32)
    for o in range(chans):
        reset_bias = jnp.where(iota((chans, 1), 0) == o, br[o], reset_bias)
    for b in range(bands):
        for side in range(2):
            at = slice((2 * side + b) * cols, (2 * side + b + 1) * cols)
            for i in range(2):
                held = (got_up[b, 1 + i] if side == 0 else got_dn[b, i]).astype(F32)
                reset = sigmoid(acc[i * chans : (i + 1) * chans, at] + reset_bias)
                joined = jnp.concatenate([reset * held[:chans], held[chans:]], axis=0).astype(BF16)
                if side == 0:
                    gbots[slots, b, i] = joined
                else:
                    gtops[slots, b, i] = joined

    def renew(s, pooled):
        above, below = place(s, 0), place(s, 1)
        for b in range(bands):
            at = slice(b * cols, (b + 1) * cols)
            x = jnp.concatenate([gbots[above, b, 0], gbots[above, b, 1], gtops[below, b, 0], gtops[below, b, 1]], axis=0)
            for j, step in enumerate((-1, 0, 1)):
                x2[s, j * k2 + km : (j + 1) * k2, at] = shifted(x, 2 * step) if step else x
        acc = jnp.dot(t2[...], x2[s], preferred_element_type=F32)
        scale = live[s].astype(F32)
        summed = []
        for o in range(half):
            both = None
            for b in range(bands):
                at = slice(b * cols, (b + 1) * cols)
                update = gates[s, b, o * rows : (o + 1) * rows]
                cand = jnp.tanh(acc[o * rows : (o + 1) * rows, at] + bc[start + o])
                held = state[b, s, pl.ds(pl.multiple_of((start + o) * rows, rows), rows), :]
                new = ((1.0 - update) * held + update * cand) * scale
                out[b, s, o] = new
                both = new if both is None else both + new
            summed.append(both)
        summed = jnp.concatenate(summed, axis=0)
        spot = jnp.int32(0)
        for k in range(slots):
            spot = jnp.where(perm[0, k] == s, k, spot)
        gather = jnp.where(
            iota((cols, slots * cw), 1) == spot * cw + (iota((cols, slots * cw), 0) >> 2), 1.0 / 16.0, 0.0
        )
        product = jnp.dot(jnp.concatenate(thirds(summed), axis=0), gather.astype(BF16), preferred_element_type=F32)
        pooled = pooled + (product[:mu] + (product[mu : 2 * mu] + product[2 * mu :]))
        return pooled

    pooled = lax.fori_loop(0, slots, renew, jnp.zeros((mu, slots * cw), F32))

    m, q = iota((cr * half, mu), 0), iota((cr * half, mu), 1)
    rowsum = jnp.where(((m & (half - 1)) == (q >> 4)) & ((m >> (half.bit_length() - 1)) == ((q & (rows - 1)) >> 2)), 1.0, 0.0)
    product = jnp.dot(rowsum.astype(BF16), jnp.concatenate(thirds(pooled), axis=1), preferred_element_type=F32)
    parts[me] = product[:, :cols] + (product[:, cols : 2 * cols] + product[:, 2 * cols :])

    copies = []
    for d in range(1, npeer):
        peer = lax.rem(me + d, npeer)
        copy = pltpu.make_async_remote_copy(
            parts.at[me], parts.at[me], pool_send.at[d - 1], pool_recv.at[d - 1],
            device_id={"band": peer // nr, "rep": lax.rem(peer, nr)}, device_id_type=MESH,
        )
        copy.start()
        copies.append(copy)
    for copy in copies:
        copy.wait()


def finish(
    nb, nr, own, parts, coarse, u_pool, new_in, out, coarse_out, cout, store_sems
):
    bands, slots, half = new_in.shape[:3]
    cr, cw = cout.shape[2], cout.shape[3]
    cols = slots * cw
    band = lax.axis_index("band")
    stores = []
    for b in range(bands):
        for s in range(slots):
            stores.append(pltpu.make_async_copy(new_in.at[b, s], out.at[b, s], store_sems.at[b * slots + s]))
            stores[-1].start()
    halves = []
    for r in range(nr):
        total = parts[r]
        for b in range(1, nb):
            total = total + parts[b * nr + r]
        halves.append(pltpu.roll(total, lax.rem(cols - band * (own * cw), cols), 1))
    wide = jnp.concatenate(
        [jnp.concatenate([x[i * half : (i + 1) * half] for x in halves], axis=0) for i in range(cr)], axis=1
    )
    pre = coarse[1] + jnp.dot(u_pool[...], wide, precision=HIGHEST, preferred_element_type=F32)
    new = coarse[0] + jnp.tanh(pre)
    for k in range(own):
        for i in range(cr):
            cout[k, :, i, :] = new[:, i * cols + k * cw : i * cols + (k + 1) * cw]
    stores.append(pltpu.make_async_copy(cout, coarse_out, store_sems.at[bands * slots]))
    stores[-1].start()
    for store in stores:
        store.wait()


def shards(nt, nb, nr, features, state, live, nbrs, perm, cs, wu, bu, wr, br, wc, bc, u_pool, u_state, b_coarse):
    bands, slots, chans, rows, cols = state.shape
    ins = features.shape[2]
    width = ins + chans
    half = chans // nr
    km = width * rows
    slab = 32
    k1, k2, k3 = 3 * (km + 2 * slab), 3 * (km + 4 * slab), 12 * slab
    cr = rows // 4
    hbm = pl.BlockSpec(memory_space=pltpu.HBM)
    vm = pl.BlockSpec(memory_space=pltpu.VMEM)
    features = features.reshape(bands, slots, ins * rows, cols)
    state = state.reshape(bands, slots, chans * rows, cols)
    big = tuple(
        pltpu.with_memory_space_constraint(x, pltpu.HBM) for x in (features, state, cs, wu, wr, wc, u_state)
    )
    small = tuple(
        pltpu.with_memory_space_constraint(x, pltpu.HBM) for x in (live, nbrs.T, perm, bu, br, bc, b_coarse)
    )
    fine = jax.ShapeDtypeStruct((bands, slots, half, rows, cols), F32)
    pooled = jax.ShapeDtypeStruct((nb * nr, cr * half, cols), F32)
    coarse = jax.ShapeDtypeStruct((2, chans, cr * cols), F32)
    new, parts, held = pl.pallas_call(
        functools.partial(kernel, nt, nb, nr, ins, rows),
        out_shape=(fine, pooled, coarse),
        in_specs=[hbm] * (len(small) + len(big)),
        out_specs=(vm, vm, vm),
        scratch_shapes=[pltpu.SMEM(x.shape, x.dtype) for x in small]
        + [pltpu.VMEM(x.shape, x.dtype) for x in big]
        + [
            pltpu.VMEM((bands, slots, ins * rows, cols), F32),
            pltpu.VMEM((bands, 3, slab, cols), BF16),
            pltpu.VMEM((bands, 3, slab, cols), BF16),
            pltpu.VMEM((bands, 3, slab, cols), BF16),
            pltpu.VMEM((bands, 3, slab, cols), BF16),
            pltpu.VMEM((slots + 2, bands, slab, cols), BF16),
            pltpu.VMEM((slots + 2, bands, slab, cols), BF16),
            pltpu.VMEM((slots + 2, bands, 2, slab, cols), BF16),
            pltpu.VMEM((slots + 2, bands, 2, slab, cols), BF16),
            pltpu.VMEM((k3, 2 * bands * cols), BF16),
            pltpu.VMEM((slots, bands, (half + chans) * rows, cols), F32),
            pltpu.VMEM((6, chans, k1), F32),
            pltpu.VMEM((3, chans, k2), F32),
            pltpu.VMEM((3, chans, k3), F32),
            pltpu.VMEM(((half + chans) * rows, k1), BF16),
            pltpu.VMEM((half * rows, k2), BF16),
            pltpu.VMEM((2 * chans, k3), BF16),
            pltpu.VMEM((slots, k1, bands * cols), BF16),
            pltpu.VMEM((slots, k2, bands * cols), BF16),
            pltpu.SemaphoreType.DMA((len(small) + len(big) + bands * slots,)),
            pltpu.SemaphoreType.DMA((2,)),
            pltpu.SemaphoreType.DMA((2,)),
            pltpu.SemaphoreType.DMA((nb * nr - 1,)),
            pltpu.SemaphoreType.DMA((nb * nr - 1,)),
        ],
        compiler_params=pltpu.CompilerParams(
            collective_id=0, has_side_effects=True, vmem_limit_bytes=24 * 1024 * 1024
        ),
    )(*small, *big)
    return pl.pallas_call(
        functools.partial(finish, nb, nr, cs.shape[0]),
        out_shape=(fine, jax.ShapeDtypeStruct(cs.shape, F32)),
        in_specs=[vm, vm, vm, pl.BlockSpec(memory_space=pl.ANY)],
        out_specs=(hbm, hbm),
        scratch_shapes=[
            pltpu.VMEM(cs.shape, F32),
            pltpu.SemaphoreType.DMA((bands * slots + 1,)),
        ],
        compiler_params=pltpu.CompilerParams(vmem_limit_bytes=24 * 1024 * 1024),
    )(parts, held, u_pool, new)


def solution(mesh):
    nt, nb, nr = mesh.shape["tiles"], mesh.shape["band"], mesh.shape["rep"]
    return jax.shard_map(
        functools.partial(shards, nt, nb, nr),
        mesh=mesh,
        in_specs=(
            P(("groups", "band"), "tiles", None, None, None),
            P(("groups", "band"), "tiles", None, None, None),
            P("tiles"),
            P("tiles", None),
            P("tiles", None),
            P(("groups", "tiles", "band"), None, None, None),
            P(),
            P(),
            P(),
            P(),
            P(),
            P(),
            P(),
            P(),
            P(),
        ),
        out_specs=(
            P(("groups", "band"), "tiles", "rep", None, None),
            P(("groups", "tiles", "band"), None, None, None),
        ),
        check_vma=False,
    )
```

```python
import functools

import jax
import jax.numpy as jnp
from jax import lax
from jax.experimental import pallas as pl
from jax.experimental.pallas import tpu as pltpu
from jax.sharding import PartitionSpec as P

MESH = pl.DeviceIdType.MESH
HIGHEST = lax.Precision.HIGHEST
F32 = jnp.float32
BF16 = jnp.bfloat16


def iota(shape, dim):
    return lax.broadcasted_iota(jnp.int32, shape, dim)


def sigmoid(x):
    return 0.5 * jnp.tanh(0.5 * x) + 0.5


def thirds(x):
    high = x.astype(BF16)
    rest = x - high.astype(F32)
    middle = rest.astype(BF16)
    return high, middle, (rest - middle.astype(F32)).astype(BF16)


def shifted(x, step):
    width = x.shape[1]
    wide = pltpu.roll(x, (-step) % width, 1).reshape(-1, 16, width)
    column = iota((16, width), 1) + step
    keep = ((column >= 0) & (column < width)).astype(F32).astype(BF16)
    return (wide * keep[None]).reshape(x.shape)


def kernel(
    nt, nb, nr, ins, rows,
    live_in, nbrs_in, perm_in, bu_in, br_in, bc_in, b_coarse_in, features_in, state_in, cs_in, wu_in, wr_in, wc_in, u_state_in,
    out, parts, coarse,
    live, nbrs, perm, bu, br, bc, b_coarse, features, state, cs, wu, wr, wc, u_state,
    feats, send_up, send_dn, got_up, got_dn, tops, bots, gtops, gbots, strip, gates,
    w1, wh, w2, w3, t1, th, t2, t3, x1, xh, x2, sums,
    load_sems, up_sems, dn_sems, pool_send, pool_recv,
):
    bands, slots, flat, cols = state.shape
    chans = flat // rows
    half = chans // nr
    width = ins + chans
    own, cr, cw = cs.shape[0], cs.shape[2], cs.shape[3]
    km = width * rows
    slab = strip.shape[0] // 12
    tile = lax.axis_index("tiles")
    band = lax.axis_index("band")
    rep = lax.axis_index("rep")
    base = tile * slots
    npeer = nb * nr
    me = band * nr + rep
    start = rep * half

    loads = [
        pltpu.make_async_copy(src, dst, load_sems.at[i])
        for i, (src, dst) in enumerate(
            (
                (wu_in, wu), (wr_in, wr), (wc_in, wc), (features_in, features),
                (cs_in, cs), (u_state_in, u_state),
                (live_in, live), (nbrs_in, nbrs), (perm_in, perm),
                (bu_in, bu), (br_in, br), (bc_in, bc), (b_coarse_in, b_coarse),
            )
        )
    ]
    state_loads = [
        pltpu.make_async_copy(state_in.at[b, s], state.at[b, s], load_sems.at[len(loads) + b * slots + s])
        for b in range(bands)
        for s in range(slots)
    ]
    for load in loads[:4] + state_loads + loads[4:]:
        load.start()

    barrier = pltpu.get_barrier_semaphore()
    has_up, has_dn = tile > 0, tile < nt - 1

    @pl.when(has_up)
    def _():
        pl.semaphore_signal(barrier, inc=1, device_id={"tiles": tile - 1}, device_id_type=MESH)

    @pl.when(has_dn)
    def _():
        pl.semaphore_signal(barrier, inc=1, device_id={"tiles": tile + 1}, device_id_type=MESH)

    for d in range(1, npeer):
        peer = lax.rem(me + d, npeer)
        pl.semaphore_signal(
            barrier, inc=1, device_id={"band": peer // nr, "rep": lax.rem(peer, nr)}, device_id_type=MESH
        )

    def lanes(size, main, halo):
        part = size // 3
        k = iota((1, size), 1)
        side = (k >= part).astype(jnp.int32) + (k >= 2 * part).astype(jnp.int32)
        q = k - part * side
        h = q - main
        chan = jnp.where(h >= 0, h & (slab - 1), q >> 4)
        row = q & (rows - 1)
        for j, at in enumerate(halo):
            row = jnp.where(h >= j * slab, at, row)
        entry = jnp.where(chan < chans, chan + ins, chan - chans)
        return jnp.where(chan < width, entry + 32 * side, -1), row

    def spread(target, weights, main, halo):
        size = target.shape[2]
        entry, _ = lanes(size, main, halo)
        total = jnp.zeros((3 * chans * len(weights), size), F32)
        for b in range(3):
            stack = jnp.concatenate([w[3 * a + b] for w in weights for a in range(3)], axis=0)
            pick = (entry == iota((width, size), 0) + 32 * b).astype(F32).astype(BF16)
            total = total + jnp.dot(stack, pick, preferred_element_type=F32)
        target[...] = total.reshape(target.shape)

    def fill(target, source, jobs, main, halo, dilation):
        shape = (rows, target.shape[1])
        _, row = lanes(shape[1], main, halo)
        delta = row - iota(shape, 0)
        hits = [(delta == a * dilation).astype(F32).astype(BF16) for a in (-1, 0, 1)]
        for at, gate, outs, count in jobs:
            for o in range(count):
                total = None
                for a in range(3):
                    line = jnp.broadcast_to(source[3 * gate + a, pl.ds(outs + o, 1), :], shape).astype(BF16)
                    total = line * hits[a] if total is None else total + line * hits[a]
                target[at + o * rows : at + (o + 1) * rows, :] = total

    mu = half * rows
    halo1, halo2, halo3 = (-1, rows), (-2, -1, rows, rows + 1), (-3, -2, -1, 0)
    for load in loads[:3]:
        load.wait()
    spread(w1, (wu, wr), km, ())
    spread(wh, (wu, wr), 0, halo1)
    spread(w2, (wc,), km, halo2)
    spread(w3, (wr,), 0, halo3)
    for load in loads[6:]:
        load.wait()
    first = jnp.int32(0)
    last = jnp.int32(0)
    for s in range(slots):
        u, d = nbrs[0, s], nbrs[1, s]
        alive = live[s] > 0
        first = jnp.where(alive & ((u < base) | (u >= base + slots)), s, first)
        last = jnp.where(alive & ((d < base) | (d >= base + slots)), s, last)

    for load in loads[3:4] + state_loads:
        load.wait()
    for s in range(slots):
        for b in range(bands):
            feats[b, s] = features[b, s].astype(F32)

    blank = jnp.zeros((slab - width, cols), F32)

    def feat_rows(b, s, row):
        return jnp.concatenate([feats[b, s, ch * rows + row : ch * rows + row + 1] for ch in range(ins)] + [blank], axis=0)

    def row_slab(b, s, row):
        return jnp.concatenate([state[b, s, pl.ds(row, chans, stride=rows), :], feat_rows(b, s, row)], axis=0).astype(BF16)

    for b in range(bands):
        for i in range(3):
            send_up[b, i] = row_slab(b, first, i)
            send_dn[b, i] = row_slab(b, last, rows - 3 + i)

    pl.semaphore_wait(barrier, npeer - 1 + jnp.where(has_up, 1, 0) + jnp.where(has_dn, 1, 0))

    def copy_up():
        return pltpu.make_async_remote_copy(
            send_up, got_dn, up_sems.at[0], up_sems.at[1], device_id={"tiles": tile - 1}, device_id_type=MESH
        )

    def copy_dn():
        return pltpu.make_async_remote_copy(
            send_dn, got_up, dn_sems.at[0], dn_sems.at[1], device_id={"tiles": tile + 1}, device_id_type=MESH
        )

    @pl.when(has_up)
    def _():
        copy_up().start()

    @pl.when(has_dn)
    def _():
        copy_dn().start()

    @pl.when(jnp.logical_not(has_up))
    def _():
        got_up[...] = jnp.zeros_like(got_up)

    @pl.when(jnp.logical_not(has_dn))
    def _():
        got_dn[...] = jnp.zeros_like(got_dn)

    fill(t1, w1, ((0, 0, start, half), (mu, 1, 0, chans)), km, (), 1)
    fill(th, wh, ((0, 0, start, half), (mu, 1, 0, chans)), 0, halo1, 1)
    fill(t2, w2, ((0, 0, start, half),), km, halo2, 2)
    _, row3 = lanes(t3.shape[1], 0, halo3)
    for i in range(2):
        total = jnp.zeros((chans, t3.shape[1]), F32)
        for a in range(3):
            total = jnp.where(row3 == i - 2 + a - 1, w3[a], total)
        t3[i * chans : (i + 1) * chans] = total.astype(BF16)

    for load in loads[4:6]:
        load.wait()
    coarse[0] = jnp.zeros_like(coarse[0])
    for k in range(own):
        for i in range(cr):
            coarse[0, :, i * cols + k * cw : i * cols + (k + 1) * cw] = cs[k, :, i, :]
    coarse_bias = jnp.zeros((chans, 1), F32)
    for o in range(chans):
        coarse_bias = jnp.where(iota((chans, 1), 0) == o, b_coarse[o], coarse_bias)
    coarse[1] = jnp.dot(u_state[...], coarse[0], precision=HIGHEST, preferred_element_type=F32) + coarse_bias

    k1, kh, k2 = km, 2 * slab, km + 4 * slab
    for s in range(slots):
        for b in range(bands):
            at = slice(b * cols, (b + 1) * cols)
            tops[s, b] = row_slab(b, s, 0)
            bots[s, b] = row_slab(b, s, rows - 1)
            x = state[b, s].astype(BF16)
            f = features[b, s]
            for j, step in enumerate((-1, 0, 1)):
                x1[s, j * k1 : j * k1 + flat, at] = shifted(x, step) if step else x
                x1[s, j * k1 + flat : j * k1 + km, at] = shifted(f, step) if step else f
                x2[s, j * k2 + flat : j * k2 + km, at] = shifted(f, 2 * step) if step else f
        sums[s] = jnp.dot(t1[...], x1[s], preferred_element_type=F32)
    tops[slots + 1] = jnp.zeros((bands, slab, cols), BF16)
    bots[slots + 1] = jnp.zeros((bands, slab, cols), BF16)
    gtops[slots + 1] = jnp.zeros((bands, 2, slab, cols), BF16)
    gbots[slots + 1] = jnp.zeros((bands, 2, slab, cols), BF16)
    edge_up = [row_slab(b, first, 0) for b in range(bands)]
    edge_dn = [row_slab(b, last, rows - 1) for b in range(bands)]

    @pl.when(has_up)
    def _():
        copy_up().wait_send()

    @pl.when(has_dn)
    def _():
        copy_up().wait_recv()

    @pl.when(has_dn)
    def _():
        copy_dn().wait_send()

    @pl.when(has_up)
    def _():
        copy_dn().wait_recv()

    for b in range(bands):
        bots[slots, b] = got_up[b, 2]
        tops[slots, b] = got_dn[b, 0]

    def place(s, side):
        n = nbrs[side, s]
        here = (n >= base) & (n < base + slots)
        return jnp.where(here, n - base, jnp.where(n >= 0, slots, slots + 1))

    updates = []
    for s in range(slots):
        above, below = place(s, 0), place(s, 1)
        for b in range(bands):
            at = slice(b * cols, (b + 1) * cols)
            x = jnp.concatenate([bots[above, b], tops[below, b]], axis=0)
            for j, step in enumerate((-1, 0, 1)):
                xh[s, j * kh : (j + 1) * kh, at] = shifted(x, step) if step else x
        acc = sums[s] + jnp.dot(th[...], xh[s], preferred_element_type=F32)
        for b in range(bands):
            at = slice(b * cols, (b + 1) * cols)
            for o in range(half):
                gates[s, b, o * rows : (o + 1) * rows] = sigmoid(acc[o * rows : (o + 1) * rows, at] + bu[start + o])
            for o in range(chans):
                reset = sigmoid(acc[mu + o * rows : mu + (o + 1) * rows, at] + br[o])
                held = state[b, s, o * rows : (o + 1) * rows].astype(BF16).astype(F32)
                gates[s, b, mu + o * rows : mu + (o + 1) * rows] = reset * held
            x = gates[s, b, mu:].astype(BF16)
            for j, step in enumerate((-1, 0, 1)):
                x2[s, j * k2 : j * k2 + flat, at] = shifted(x, 2 * step) if step else x
            for i in range(2):
                for target, row in ((gtops, i), (gbots, rows - 2 + i)):
                    g = gates[s, b, pl.ds(mu + row, chans, stride=rows), :]
                    target[s, b, i] = jnp.concatenate([g, feat_rows(b, s, row)], axis=0).astype(BF16)

    for b in range(bands):
        for side in range(2):
            four = [got_up[b, i] for i in range(3)] + [edge_up[b]] if side == 0 else [edge_dn[b]] + [got_dn[b, i] for i in range(3)]
            at = slice((2 * side + b) * cols, (2 * side + b + 1) * cols)
            x = jnp.concatenate(four, axis=0)
            strip[0 : 4 * slab, at] = shifted(x, -1)
            strip[4 * slab : 8 * slab, at] = x
            strip[8 * slab :, at] = shifted(x, 1)
    acc = jnp.dot(t3[...], strip[...], preferred_element_type=F32)
    reset_bias = jnp.zeros((chans, 1), F32)
    for o in range(chans):
        reset_bias = jnp.where(iota((chans, 1), 0) == o, br[o], reset_bias)
    for b in range(bands):
        for side in range(2):
            at = slice((2 * side + b) * cols, (2 * side + b + 1) * cols)
            for i in range(2):
                held = (got_up[b, 1 + i] if side == 0 else got_dn[b, i]).astype(F32)
                reset = sigmoid(acc[i * chans : (i + 1) * chans, at] + reset_bias)
                joined = jnp.concatenate([reset * held[:chans], held[chans:]], axis=0).astype(BF16)
                if side == 0:
                    gbots[slots, b, i] = joined
                else:
                    gtops[slots, b, i] = joined

    pooled = jnp.zeros((mu, slots * cw), F32)
    for s in range(slots):
        above, below = place(s, 0), place(s, 1)
        for b in range(bands):
            at = slice(b * cols, (b + 1) * cols)
            x = jnp.concatenate([gbots[above, b, 0], gbots[above, b, 1], gtops[below, b, 0], gtops[below, b, 1]], axis=0)
            for j, step in enumerate((-1, 0, 1)):
                x2[s, j * k2 + km : (j + 1) * k2, at] = shifted(x, 2 * step) if step else x
        acc = jnp.dot(t2[...], x2[s], preferred_element_type=F32)
        scale = live[s].astype(F32)
        summed = []
        for o in range(half):
            both = None
            for b in range(bands):
                at = slice(b * cols, (b + 1) * cols)
                update = gates[s, b, o * rows : (o + 1) * rows]
                cand = jnp.tanh(acc[o * rows : (o + 1) * rows, at] + bc[start + o])
                held = state[b, s, pl.ds(pl.multiple_of((start + o) * rows, rows), rows), :]
                new = ((1.0 - update) * held + update * cand) * scale
                out[b, s, o] = new
                both = new if both is None else both + new
            summed.append(both)
        summed = jnp.concatenate(summed, axis=0)
        spot = jnp.int32(0)
        for k in range(slots):
            spot = jnp.where(perm[0, k] == s, k, spot)
        gather = jnp.where(
            iota((cols, slots * cw), 1) == spot * cw + (iota((cols, slots * cw), 0) >> 2), 1.0 / 16.0, 0.0
        )
        product = jnp.dot(jnp.concatenate(thirds(summed), axis=0), gather.astype(BF16), preferred_element_type=F32)
        pooled = pooled + (product[:mu] + (product[mu : 2 * mu] + product[2 * mu :]))

    m, q = iota((cr * half, mu), 0), iota((cr * half, mu), 1)
    rowsum = jnp.where(((m & (half - 1)) == (q >> 4)) & ((m >> (half.bit_length() - 1)) == ((q & (rows - 1)) >> 2)), 1.0, 0.0)
    product = jnp.dot(rowsum.astype(BF16), jnp.concatenate(thirds(pooled), axis=1), preferred_element_type=F32)
    parts[me] = product[:, :cols] + (product[:, cols : 2 * cols] + product[:, 2 * cols :])

    copies = []
    for d in range(1, npeer):
        peer = lax.rem(me + d, npeer)
        copy = pltpu.make_async_remote_copy(
            parts.at[me], parts.at[me], pool_send.at[d - 1], pool_recv.at[d - 1],
            device_id={"band": peer // nr, "rep": lax.rem(peer, nr)}, device_id_type=MESH,
        )
        copy.start()
        copies.append(copy)
    for copy in copies:
        copy.wait()


def finish(
    nb, nr, own, parts, coarse, u_pool, new_in, out, coarse_out, cout, store_sems
):
    bands, slots, half = new_in.shape[:3]
    cr, cw = cout.shape[2], cout.shape[3]
    cols = slots * cw
    band = lax.axis_index("band")
    stores = []
    for b in range(bands):
        for s in range(slots):
            stores.append(pltpu.make_async_copy(new_in.at[b, s], out.at[b, s], store_sems.at[b * slots + s]))
            stores[-1].start()
    halves = []
    for r in range(nr):
        total = parts[r]
        for b in range(1, nb):
            total = total + parts[b * nr + r]
        halves.append(pltpu.roll(total, lax.rem(cols - band * (own * cw), cols), 1))
    wide = jnp.concatenate(
        [jnp.concatenate([x[i * half : (i + 1) * half] for x in halves], axis=0) for i in range(cr)], axis=1
    )
    pre = coarse[1] + jnp.dot(u_pool[...], wide, precision=HIGHEST, preferred_element_type=F32)
    new = coarse[0] + jnp.tanh(pre)
    for k in range(own):
        for i in range(cr):
            cout[k, :, i, :] = new[:, i * cols + k * cw : i * cols + (k + 1) * cw]
    stores.append(pltpu.make_async_copy(cout, coarse_out, store_sems.at[bands * slots]))
    stores[-1].start()
    for store in stores:
        store.wait()


def shards(nt, nb, nr, features, state, live, nbrs, perm, cs, wu, bu, wr, br, wc, bc, u_pool, u_state, b_coarse):
    bands, slots, chans, rows, cols = state.shape
    ins = features.shape[2]
    width = ins + chans
    half = chans // nr
    km = width * rows
    slab = 32
    k1, kh, k2, k3 = 3 * km, 6 * slab, 3 * (km + 4 * slab), 12 * slab
    cr = rows // 4
    hbm = pl.BlockSpec(memory_space=pltpu.HBM)
    vm = pl.BlockSpec(memory_space=pltpu.VMEM)
    features = features.reshape(bands, slots, ins * rows, cols)
    state = state.reshape(bands, slots, chans * rows, cols)
    big = tuple(
        pltpu.with_memory_space_constraint(x, pltpu.HBM) for x in (features, state, cs, wu, wr, wc, u_state)
    )
    small = tuple(
        pltpu.with_memory_space_constraint(x, pltpu.HBM) for x in (live, nbrs.T, perm, bu, br, bc, b_coarse)
    )
    fine = jax.ShapeDtypeStruct((bands, slots, half, rows, cols), F32)
    pooled = jax.ShapeDtypeStruct((nb * nr, cr * half, cols), F32)
    coarse = jax.ShapeDtypeStruct((2, chans, cr * cols), F32)
    new, parts, held = pl.pallas_call(
        functools.partial(kernel, nt, nb, nr, ins, rows),
        out_shape=(fine, pooled, coarse),
        in_specs=[hbm] * (len(small) + len(big)),
        out_specs=(vm, vm, vm),
        scratch_shapes=[pltpu.SMEM(x.shape, x.dtype) for x in small]
        + [pltpu.VMEM(x.shape, x.dtype) for x in big]
        + [
            pltpu.VMEM((bands, slots, ins * rows, cols), F32),
            pltpu.VMEM((bands, 3, slab, cols), BF16),
            pltpu.VMEM((bands, 3, slab, cols), BF16),
            pltpu.VMEM((bands, 3, slab, cols), BF16),
            pltpu.VMEM((bands, 3, slab, cols), BF16),
            pltpu.VMEM((slots + 2, bands, slab, cols), BF16),
            pltpu.VMEM((slots + 2, bands, slab, cols), BF16),
            pltpu.VMEM((slots + 2, bands, 2, slab, cols), BF16),
            pltpu.VMEM((slots + 2, bands, 2, slab, cols), BF16),
            pltpu.VMEM((k3, 2 * bands * cols), BF16),
            pltpu.VMEM((slots, bands, (half + chans) * rows, cols), F32),
            pltpu.VMEM((6, chans, k1), F32),
            pltpu.VMEM((6, chans, kh), F32),
            pltpu.VMEM((3, chans, k2), F32),
            pltpu.VMEM((3, chans, k3), F32),
            pltpu.VMEM(((half + chans) * rows, k1), BF16),
            pltpu.VMEM(((half + chans) * rows, kh), BF16),
            pltpu.VMEM((half * rows, k2), BF16),
            pltpu.VMEM((2 * chans, k3), BF16),
            pltpu.VMEM((slots, k1, bands * cols), BF16),
            pltpu.VMEM((slots, kh, bands * cols), BF16),
            pltpu.VMEM((slots, k2, bands * cols), BF16),
            pltpu.VMEM((slots, (half + chans) * rows, bands * cols), F32),
            pltpu.SemaphoreType.DMA((len(small) + len(big) + bands * slots,)),
            pltpu.SemaphoreType.DMA((2,)),
            pltpu.SemaphoreType.DMA((2,)),
            pltpu.SemaphoreType.DMA((nb * nr - 1,)),
            pltpu.SemaphoreType.DMA((nb * nr - 1,)),
        ],
        compiler_params=pltpu.CompilerParams(
            collective_id=0, has_side_effects=True, vmem_limit_bytes=24 * 1024 * 1024
        ),
    )(*small, *big)
    return pl.pallas_call(
        functools.partial(finish, nb, nr, cs.shape[0]),
        out_shape=(fine, jax.ShapeDtypeStruct(cs.shape, F32)),
        in_specs=[vm, vm, vm, pl.BlockSpec(memory_space=pl.ANY)],
        out_specs=(hbm, hbm),
        scratch_shapes=[
            pltpu.VMEM(cs.shape, F32),
            pltpu.SemaphoreType.DMA((bands * slots + 1,)),
        ],
        compiler_params=pltpu.CompilerParams(vmem_limit_bytes=24 * 1024 * 1024),
    )(parts, held, u_pool, new)


def solution(mesh):
    nt, nb, nr = mesh.shape["tiles"], mesh.shape["band"], mesh.shape["rep"]
    return jax.shard_map(
        functools.partial(shards, nt, nb, nr),
        mesh=mesh,
        in_specs=(
            P(("groups", "band"), "tiles", None, None, None),
            P(("groups", "band"), "tiles", None, None, None),
            P("tiles"),
            P("tiles", None),
            P("tiles", None),
            P(("groups", "tiles", "band"), None, None, None),
            P(),
            P(),
            P(),
            P(),
            P(),
            P(),
            P(),
            P(),
            P(),
        ),
        out_specs=(
            P(("groups", "band"), "tiles", "rep", None, None),
            P(("groups", "tiles", "band"), None, None, None),
        ),
        check_vma=False,
    )
```
